128 devices in a mesh: rep: 4 (over z), emb: 32 (over y, x, core).
Axes of the slice: x: 4, y: 4, z: 4, core: 2. Of those that a mesh axis runs over, the one named last changes fastest.
Arguments:
- tables: bfloat16 [800, 1024, 128], P('emb'), may hold values from -2 to 2
- bag_ids: int32 [800, 1024, 16], P('emb', 'rep'), may hold values from 0 to 1023
- bag_lengths: int32 [800, 1024], P('emb', 'rep'), may hold values from 1 to 16
- field_slot: int32 [800], replicated, may hold values from 0 to 799, each once
- pair_blocks: int32 [64, 2], replicated, may hold values from 0 to 99, as said below
- w_over: bfloat16 [4096, 4096], P(None, 'emb'), may hold values from -0.09375 to 0.09375
- b_over: bfloat16 [4096], P('emb'), may hold values from -3 to 3
- cotangent: bfloat16 [1024, 4096], P('rep', 'emb'), may hold values from -6 to 6
Outputs:
- over_out: bfloat16 [1024, 4096], P('rep', 'emb')
- grad_w: float32 [4096, 4096], P(None, 'emb')
- grad_b: float32 [4096], P('emb')
- pooled_grad: bfloat16 [800, 1024, 128], P('emb', 'rep')
The draws below stay inside these ranges and needn't reach their ends.
Inputs may be any that keep to these rules, and one draw needn't show every extreme that they name: `pair_blocks`: each row names two field blocks, possibly equal; every block appears in some row.
All inputs are finite; a program needn't handle non-finite values.
Results may differ from the reference program's by a relative error of at most 0.0073.
Values may be sent and summed in bfloat16 or wider, within the bound.
A program may use at most 128 MiB of HBM per device.

```python
import math
import jax
import jax.numpy as jnp
import numpy as np
from jax import lax

E = 128
H = 4096
BLK = 8
NPAIR = 64
BAG = 16
ROWS = 1024
FEATURES = 800
NBLK = 100
INTER = 4096
SAMPLES = 1024


def draw_pair_blocks(key, part):
    key = jax.random.fold_in(key, 7)
    key_off, key_rand, key_perm = jax.random.split(key, 3)
    offset = jax.random.randint(key_off, (), 0, NBLK)
    index = jnp.arange(NPAIR, dtype=jnp.int32)
    first = (index + offset) % NBLK
    shifted = (index + NPAIR + offset) % NBLK
    random_second = jax.random.randint(key_rand, (NPAIR,), 0, NBLK)
    second = jnp.where(index < NBLK - NPAIR, shifted, random_second)
    pairs = jnp.stack([first, second], axis=1)
    order = jax.random.permutation(key_perm, NPAIR)
    return pairs[order].astype(jnp.int32)


def plant(drawn, stream_key, least, high):
    place = [jax.random.randint(jax.random.fold_in(stream_key, axis), (), 0, length) for axis, length in enumerate(drawn.shape)]
    main_axis = drawn.shape.index(max(drawn.shape))
    next_to = place[:main_axis] + [(place[main_axis] + 1) % drawn.shape[main_axis]] + place[main_axis + 1:]
    return drawn.at[tuple(place)].set(least).at[tuple(next_to)].set(high)


def block_scale(own_key, dims, pieces, low, top_value):
    level, own = 1.0, jax.random.fold_in(own_key, 6)
    for position, parts in pieces:
        steps = jnp.exp(jax.random.uniform(jax.random.fold_in(own, position), (parts,), jnp.float32, low / len(pieces), top_value / len(pieces)))
        level = level * jnp.repeat(steps, dims[position] // parts).reshape([-1 if axis == position else 1 for axis in range(len(dims))])
    return level


def rank_table(number_of, lean):
    weights = [(1 << 20) // math.isqrt(rank ** lean) + 1 for rank in range(1, number_of + 1)]
    deviation = 1 + sum(weights) // (1 << 30)
    return np.cumsum(np.array([max(1, weight // deviation) for weight in weights]))


def ranked_ids(stream_key, dims, number_of, lean):
    listing = rank_table(number_of, lean)
    pick = jax.random.randint(jax.random.fold_in(stream_key, 1), dims, 0, int(listing[number_of - 1]))
    grade = jnp.searchsorted(jnp.asarray(listing, jnp.int32), pick, side="right")
    return jax.random.permutation(jax.random.fold_in(stream_key, 2), number_of)[grade].astype(jnp.int32)


def bell_draw(rng, dims, spread, reach, shards=(), kind=jnp.bfloat16):
    values = spread * jax.random.normal(rng, dims, jnp.float32)
    if shards:
        values = values * block_scale(rng, dims, shards, -0.22, 0.18)
    return jnp.clip(values, -reach, reach).astype(kind)


def setup_inputs(seed: int = 0) -> dict:
    keys = jax.random.split(jax.random.key(seed), 9)
    return {
        "tables": bell_draw(keys[0], (FEATURES, ROWS, E), 0.3, 2.0, ((0, 32),)),
        "bag_ids": plant(ranked_ids(keys[1], (FEATURES, SAMPLES, BAG), ROWS, 2), jax.random.fold_in(keys[1], 3), 0, ROWS - 1).astype(jnp.int32),
        "bag_lengths": plant(jax.random.randint(keys[2], (FEATURES, SAMPLES), 1, BAG + 1), jax.random.fold_in(keys[2], 1), 1, BAG).astype(jnp.int32),
        "field_slot": jax.random.permutation(keys[3], FEATURES).astype(jnp.int32),
        "pair_blocks": draw_pair_blocks(jax.random.fold_in(keys[8], 71), 0),
        "w_over": bell_draw(keys[5], (INTER, H), INTER ** -0.5, 0.09375, ((1, 32),)),
        "b_over": bell_draw(keys[6], (H,), 0.5, 3.0, ((0, 32),)),
        "cotangent": bell_draw(keys[7], (SAMPLES, H), 1.0, 6.0, ((0, 4), (1, 32))),
    }


def pool_table(item):
    table, ids, lengths = item
    positions = jnp.arange(BAG, dtype=jnp.int32)
    rows = table[ids].astype(jnp.float32)
    weights = (positions[None, :] < lengths[:, None]).astype(jnp.float32)
    return lax.optimization_barrier(jnp.sum(rows * weights[:, :, None], axis=1)).astype(jnp.bfloat16)

def reference(tables, bag_ids, bag_lengths, field_slot, pair_blocks, w_over, b_over, cotangent):
    scale = 1.0 / math.sqrt(E)
    pooled = lax.map(pool_table, (tables, bag_ids, bag_lengths))
    fields = pooled[field_slot]
    blocks = fields.reshape(NBLK, BLK, SAMPLES, E)

    def pair_gram(pair):
        left = blocks[pair[0]].astype(jnp.float32)
        right = blocks[pair[1]].astype(jnp.float32)
        return jnp.einsum('ise,jse->sij', left, right) * scale
    grams = lax.map(pair_gram, pair_blocks)
    inter = jnp.transpose(grams, (1, 0, 2, 3)).reshape(SAMPLES, INTER).astype(jnp.bfloat16)
    pre = jnp.dot(inter, w_over, preferred_element_type=jnp.float32) + b_over.astype(jnp.float32)
    over_out = jax.nn.silu(pre).astype(jnp.bfloat16)
    sig = jax.nn.sigmoid(pre)
    dpre = (cotangent.astype(jnp.float32) * sig * (1.0 + pre * (1.0 - sig))).astype(jnp.bfloat16)
    grad_w = jnp.dot(inter.T, dpre, preferred_element_type=jnp.float32)
    grad_b = lax.optimization_barrier(jnp.sum(dpre.astype(jnp.float32), axis=0))
    dinter = jnp.dot(dpre, w_over.T, preferred_element_type=jnp.float32).astype(jnp.bfloat16)
    dpairs = jnp.transpose(dinter.reshape(SAMPLES, NPAIR, BLK, BLK), (1, 0, 2, 3))

    def add_pair(index, total):
        first = pair_blocks[index, 0]
        second = pair_blocks[index, 1]
        grad_pair = dpairs[index].astype(jnp.float32)
        left = blocks[first].astype(jnp.float32)
        right = blocks[second].astype(jnp.float32)
        to_left = jnp.einsum('sij,jse->ise', grad_pair, right) * scale
        to_right = jnp.einsum('sij,ise->jse', grad_pair, left) * scale
        total = total.at[first].add(to_left)
        return total.at[second].add(to_right)
    dblocks = lax.fori_loop(0, NPAIR, add_pair, jnp.zeros((NBLK, BLK, SAMPLES, E), jnp.float32))
    dfields = dblocks.reshape(FEATURES, SAMPLES, E).astype(jnp.bfloat16)
    pooled_grad = jnp.zeros((FEATURES, SAMPLES, E), jnp.bfloat16).at[field_slot].set(dfields)
    return (over_out, grad_w, grad_b, pooled_grad)
```

```python
import math

import jax
import jax.numpy as jnp
from jax import lax
from jax.experimental import pallas as pl
from jax.experimental.pallas import tpu as pltpu
from jax.sharding import PartitionSpec as P

BLK = 8
NPAIR = 64
GROUP = 4
WORDS = 176
BITS = 5


def pool_kernel(ids_ref, len_ref, table_ref, out_ref):
    bag, samples = ids_ref.shape[1], ids_ref.shape[2]
    rows, embed = table_ref.shape[1], table_ref.shape[2]
    ids = ids_ref[0]
    used = lax.broadcasted_iota(jnp.int32, (bag, samples), 0) < len_ref[0]
    field = ids // WORDS
    word = ids - field * WORDS
    value = jnp.where(used, jnp.left_shift(1, field * BITS), 0)
    halves = []
    for half in range(samples // 128):
        lanes = slice(half * 128, half * 128 + 128)
        row = lax.broadcasted_iota(jnp.int32, (WORDS, 128), 0)
        total = jnp.zeros((WORDS, 128), jnp.int32)
        for k in range(bag):
            total += jnp.where(row == word[k : k + 1, lanes], value[k : k + 1, lanes], 0)
        halves.append(total)
    counts = jnp.concatenate(halves, axis=1)
    pooled = jnp.zeros((embed, samples), jnp.float32)
    start = 0
    part = 0
    while start < rows:
        size = min(WORDS, rows - start)
        mask = ((1 << BITS) - 1) << (BITS * part)
        chunk = (counts[:size] & mask).astype(jnp.float32).astype(jnp.bfloat16)
        product = lax.dot_general(
            table_ref[0, start : start + size, :],
            chunk,
            (((0,), (0,)), ((), ())),
            preferred_element_type=jnp.float32,
        )
        pooled += product * (2.0 ** (-BITS * part))
        start += size
        part += 1
    out = pooled.T.astype(jnp.bfloat16)
    out_ref[...] = out.reshape(out_ref.shape)


def pool(ids, lengths, tables, ndest):
    ntab, bag, samples = ids.shape
    rows, embed = tables.shape[1:]
    per = samples // ndest
    return pl.pallas_call(
        pool_kernel,
        grid=(ntab,),
        in_specs=[
            pl.BlockSpec((1, bag, samples), lambda t: (t, 0, 0)),
            pl.BlockSpec((1, 1, samples), lambda t: (t, 0, 0)),
            pl.BlockSpec((1, rows, embed), lambda t: (t, 0, 0)),
        ],
        out_specs=pl.BlockSpec((ndest, 1, per, embed), lambda t: (0, t, 0, 0)),
        out_shape=jax.ShapeDtypeStruct((ndest, ntab, per, embed), jnp.bfloat16),
        compiler_params=pltpu.CompilerParams(vmem_limit_bytes=48 << 20),
        name="pool",
    )(ids, lengths.reshape(ntab, 1, samples), tables)


def group_masks(samples):
    n = GROUP * BLK * samples
    r = lax.broadcasted_iota(jnp.int32, (n, n), 0)
    c = lax.broadcasted_iota(jnp.int32, (n, n), 1)
    per = BLK * samples
    same = (r // per == c // per) & (r % samples == c % samples)
    return same


def select_matrix(samples, transposed):
    rows, cols = GROUP * BLK * samples, GROUP * BLK * BLK
    shape = (cols, rows) if transposed else (rows, cols)
    r = lax.broadcasted_iota(jnp.int32, shape, 1 if transposed else 0)
    c = lax.broadcasted_iota(jnp.int32, shape, 0 if transposed else 1)
    hit = (r // (BLK * samples) == c // (BLK * BLK)) & ((r // samples) % BLK == c % BLK)
    return jnp.where(hit, 1.0, 0.0).astype(jnp.bfloat16)


def own_columns(samples):
    rows, cols = GROUP * BLK * samples, GROUP * BLK * BLK
    r = lax.broadcasted_iota(jnp.int32, (rows, cols), 0)
    c = lax.broadcasted_iota(jnp.int32, (rows, cols), 1)
    return r // samples == c // BLK


def gram_kernel(slot_ref, pair_ref, pooled_ref, inter_ref, fields_ref, sel_ref):
    samples, embed = pooled_ref.shape[1:]
    nblocks = fields_ref.shape[0]
    scale = 1.0 / math.sqrt(embed)

    def gather(c, _):
        rows = [
            pooled_ref[slot_ref[c * BLK + i]].astype(jnp.float32) for i in range(BLK)
        ]
        fields_ref[c] = jnp.concatenate(rows, axis=0).astype(jnp.bfloat16)
        return 0

    lax.fori_loop(0, nblocks, gather, 0, unroll=4)
    same = group_masks(samples)
    own = own_columns(samples)
    sel_ref[...] = select_matrix(samples, False)
    width = GROUP * BLK * BLK
    for q in range(NPAIR // GROUP):
        left = jnp.concatenate(
            [fields_ref[pair_ref[2 * (q * GROUP + p)]] for p in range(GROUP)], axis=0
        )
        right = jnp.concatenate(
            [fields_ref[pair_ref[2 * (q * GROUP + p) + 1]] for p in range(GROUP)], axis=0
        )
        gram = lax.dot_general(
            left, right, (((1,), (1,)), ((), ())), preferred_element_type=jnp.float32
        )
        gram = jnp.where(same, gram * scale, 0.0).astype(jnp.bfloat16)
        spread = jnp.dot(gram, sel_ref[...], preferred_element_type=jnp.float32)
        kept = jnp.where(own, spread, 0.0).reshape(GROUP * BLK, samples, width)
        inter_ref[:, q * width : (q + 1) * width] = jnp.sum(kept, axis=0).astype(jnp.bfloat16)


def gram(pooled_all, field_slot, pair_blocks):
    nfields, samples, embed = pooled_all.shape
    nblocks = nfields // BLK
    inter = NPAIR * BLK * BLK
    width = GROUP * BLK * BLK
    return pl.pallas_call(
        gram_kernel,
        grid=(),
        in_specs=[
            pl.BlockSpec(memory_space=pltpu.SMEM),
            pl.BlockSpec(memory_space=pltpu.SMEM),
            pl.BlockSpec(memory_space=pltpu.VMEM),
        ],
        out_specs=[pl.BlockSpec(memory_space=pltpu.VMEM)] * 2,
        out_shape=[
            jax.ShapeDtypeStruct((samples, inter), jnp.bfloat16),
            jax.ShapeDtypeStruct((nblocks, BLK * samples, embed), jnp.bfloat16),
        ],
        scratch_shapes=[pltpu.VMEM((width, width), jnp.bfloat16)],
        compiler_params=pltpu.CompilerParams(vmem_limit_bytes=48 << 20),
        name="gram",
    )(field_slot, pair_blocks.reshape(-1), pooled_all)


def gram_grad_kernel(slot_ref, pair_ref, dinter_ref, fields_ref, out_ref, total_ref, sel_ref):
    samples, embed = out_ref.shape[1:]
    nblocks = fields_ref.shape[0]
    scale = 1.0 / math.sqrt(embed)
    total_ref[...] = jnp.zeros_like(total_ref)
    same = group_masks(samples)
    own = own_columns(samples)
    sel_ref[...] = select_matrix(samples, True)
    width = GROUP * BLK * BLK
    per = BLK * samples
    for q in range(NPAIR // GROUP):
        first = [pair_ref[2 * (q * GROUP + p)] for p in range(GROUP)]
        second = [pair_ref[2 * (q * GROUP + p) + 1] for p in range(GROUP)]
        left = jnp.concatenate([fields_ref[a] for a in first], axis=0)
        right = jnp.concatenate([fields_ref[b] for b in second], axis=0)
        entry = dinter_ref[:, q * width : (q + 1) * width].astype(jnp.float32)
        spread = jnp.broadcast_to(entry[None], (GROUP * BLK, samples, width))
        spread = jnp.where(own, spread.reshape(per * GROUP, width), 0.0).astype(jnp.bfloat16)
        pair = jnp.dot(spread, sel_ref[...], preferred_element_type=jnp.float32)
        pair = jnp.where(same, pair, 0.0).astype(jnp.bfloat16)
        to_left = jnp.dot(pair, right, preferred_element_type=jnp.float32) * scale
        to_right = (
            lax.dot_general(
                pair, left, (((0,), (0,)), ((), ())), preferred_element_type=jnp.float32
            )
            * scale
        )
        for p in range(GROUP):
            total_ref[first[p]] += to_left[p * per : (p + 1) * per]
            total_ref[second[p]] += to_right[p * per : (p + 1) * per]

    def scatter(c, _):
        rows = total_ref[c]
        for i in range(BLK):
            out_ref[slot_ref[c * BLK + i]] = rows[i * samples : (i + 1) * samples].astype(
                jnp.bfloat16
            )
        return 0

    lax.fori_loop(0, nblocks, scatter, 0, unroll=4)


def gram_grad(dinter, fields, field_slot, pair_blocks):
    nblocks, per, embed = fields.shape
    samples = per // BLK
    width = GROUP * BLK * BLK
    return pl.pallas_call(
        gram_grad_kernel,
        grid=(),
        in_specs=[
            pl.BlockSpec(memory_space=pltpu.SMEM),
            pl.BlockSpec(memory_space=pltpu.SMEM),
            pl.BlockSpec(memory_space=pltpu.VMEM),
            pl.BlockSpec(memory_space=pltpu.VMEM),
        ],
        out_specs=pl.BlockSpec(memory_space=pltpu.VMEM),
        out_shape=jax.ShapeDtypeStruct((nblocks * BLK, samples, embed), jnp.bfloat16),
        scratch_shapes=[
            pltpu.VMEM((nblocks, per, embed), jnp.float32),
            pltpu.VMEM((width, width), jnp.bfloat16),
        ],
        compiler_params=pltpu.CompilerParams(vmem_limit_bytes=48 << 20),
        name="gram_grad",
    )(field_slot, pair_blocks.reshape(-1), dinter, fields)


def on_device(tables, bag_ids, bag_lengths, field_slot, pair_blocks, w_over, b_over, cotangent):
    ndev = lax.axis_size("emb")
    ntab, samples_rep, embed = tables.shape[0], bag_ids.shape[1], tables.shape[2]
    samples = samples_rep // ndev
    pooled = pool(jnp.swapaxes(bag_ids, 1, 2), bag_lengths, tables, ndev)
    pooled_all = lax.all_to_all(pooled, "emb", split_axis=0, concat_axis=0, tiled=True)
    pooled_all = pooled_all.reshape(ndev * ntab, samples, embed)
    inter, fields = gram(pooled_all, field_slot, pair_blocks)
    gathered = lax.all_gather(inter, "emb", axis=0, tiled=True)
    pre = jnp.dot(gathered, w_over, preferred_element_type=jnp.float32) + b_over.astype(jnp.float32)
    over_out = jax.nn.silu(pre).astype(jnp.bfloat16)
    sig = jax.nn.sigmoid(pre)
    dpre = (cotangent.astype(jnp.float32) * sig * (1.0 + pre * (1.0 - sig))).astype(jnp.bfloat16)
    dinter = lax.psum_scatter(
        lax.dot_general(dpre, w_over, (((1,), (1,)), ((), ())), preferred_element_type=jnp.float32),
        "emb",
        scatter_dimension=0,
        tiled=True,
    ).astype(jnp.bfloat16)
    local_w = lax.dot_general(
        gathered, dpre, (((0,), (0,)), ((), ())), preferred_element_type=jnp.float32
    )
    local_b = jnp.sum(dpre.astype(jnp.float32), axis=0)
    grad_w, grad_b = lax.psum((local_w, local_b), "rep")
    dslots = gram_grad(dinter, fields, field_slot, pair_blocks)
    dslots = dslots.reshape(ndev, ntab, samples, embed)
    back = lax.all_to_all(dslots, "emb", split_axis=0, concat_axis=0, tiled=True)
    pooled_grad = jnp.swapaxes(back, 0, 1).reshape(ntab, samples_rep, embed)
    return (over_out, grad_w, grad_b, pooled_grad)


def solution(mesh):
    in_specs = (
        P("emb", None, None),
        P("emb", "rep", None),
        P("emb", "rep"),
        P(),
        P(),
        P(None, "emb"),
        P("emb"),
        P("rep", "emb"),
    )
    out_specs = (P("rep", "emb"), P(None, "emb"), P("emb"), P("emb", "rep", None))
    return jax.shard_map(
        on_device, mesh=mesh, in_specs=in_specs, out_specs=out_specs, check_vma=False
    )
```

```python
import math

import jax
import jax.numpy as jnp
from jax import lax
from jax.experimental import pallas as pl
from jax.experimental.pallas import tpu as pltpu
from jax.sharding import PartitionSpec as P

BLK = 8
NPAIR = 64
GROUP = 4
WORDS = 176
BITS = 5


MESH = pl.DeviceIdType.MESH
CHUNK = 5


def remote(src, dst, send_sem, recv_sem, device):
    return pltpu.make_async_remote_copy(
        src_ref=src,
        dst_ref=dst,
        send_sem=send_sem,
        recv_sem=recv_sem,
        device_id=device,
        device_id_type=MESH,
    )


def greet(devices):
    barrier = pltpu.get_barrier_semaphore()
    for device in devices:
        pl.semaphore_signal(barrier, inc=1, device_id=device, device_id_type=MESH)


def greet_axis(me_rep, me_emb, ndev):
    barrier = pltpu.get_barrier_semaphore()

    def step(k, _):
        pl.semaphore_signal(
            barrier, inc=1, device_id=(me_rep, lax.rem(me_emb + k, ndev)), device_id_type=MESH
        )
        return 0

    lax.fori_loop(1, ndev, step, 0)


def pooled_rows(ids_ref, len_ref, table_ref):
    bag, samples = ids_ref.shape[1], ids_ref.shape[2]
    rows, embed = table_ref.shape[1], table_ref.shape[2]
    ids = ids_ref[0]
    used = lax.broadcasted_iota(jnp.int32, (bag, samples), 0) < len_ref[0]
    field = ids // WORDS
    word = ids - field * WORDS
    value = jnp.where(used, jnp.left_shift(1, field * BITS), 0)
    halves = []
    for half in range(samples // 128):
        lanes = slice(half * 128, half * 128 + 128)
        row = lax.broadcasted_iota(jnp.int32, (WORDS, 128), 0)
        total = jnp.zeros((WORDS, 128), jnp.int32)
        for k in range(bag):
            total += jnp.where(row == word[k : k + 1, lanes], value[k : k + 1, lanes], 0)
        halves.append(total)
    counts = jnp.concatenate(halves, axis=1)
    pooled = jnp.zeros((embed, samples), jnp.float32)
    start = 0
    part = 0
    while start < rows:
        size = min(WORDS, rows - start)
        mask = ((1 << BITS) - 1) << (BITS * part)
        chunk = (counts[:size] & mask).astype(jnp.float32).astype(jnp.bfloat16)
        product = lax.dot_general(
            table_ref[0, start : start + size, :],
            chunk,
            (((0,), (0,)), ((), ())),
            preferred_element_type=jnp.float32,
        )
        pooled += product * (2.0 ** (-BITS * part))
        start += size
        part += 1
    return pooled.T.astype(jnp.bfloat16)


def pool_kernel(ids_ref, len_ref, table_ref, out_ref, rows_ref, send_sem, recv_sem, own_sem):
    ndev, ntab, per, embed = rows_ref.shape
    table = pl.program_id(0)
    me_rep, me = lax.axis_index("rep"), lax.axis_index("emb")

    @pl.when(table == 0)
    def _():
        greet_axis(me_rep, me, ndev)
        pl.semaphore_wait(pltpu.get_barrier_semaphore(), ndev - 1)

    rows = pooled_rows(ids_ref, len_ref, table_ref)
    rows_ref[:, table] = rows.reshape(ndev, per, embed)

    @pl.when(lax.rem(table, CHUNK) == CHUNK - 1)
    def _():
        start = table - (CHUNK - 1)

        def send(k, _):
            peer = lax.rem(me + k, ndev)
            remote(
                rows_ref.at[peer, pl.ds(start, CHUNK)],
                out_ref.at[pl.ds(me * ntab + start, CHUNK)],
                send_sem,
                recv_sem,
                (me_rep, peer),
            ).start()
            return 0

        lax.fori_loop(1, ndev, send, 0)

    @pl.when(table == ntab - 1)
    def _():
        own = pltpu.make_async_copy(rows_ref.at[me], out_ref.at[pl.ds(me * ntab, ntab)], own_sem)
        own.start()
        own.wait()
        others = out_ref.at[pl.ds(0, (ndev - 1) * ntab)]
        both = remote(others, others, send_sem, recv_sem, (me_rep, lax.rem(me + 1, ndev)))
        both.wait_recv()
        both.wait_send()


def pool(ids, lengths, tables, ndev):
    ntab, bag, samples = ids.shape
    rows, embed = tables.shape[1:]
    per = samples // ndev
    return pl.pallas_call(
        pool_kernel,
        grid=(ntab,),
        in_specs=[
            pl.BlockSpec((1, bag, samples), lambda t: (t, 0, 0)),
            pl.BlockSpec((1, 1, samples), lambda t: (t, 0, 0)),
            pl.BlockSpec((1, rows, embed), lambda t: (t, 0, 0)),
        ],
        out_specs=pl.BlockSpec(memory_space=pl.ANY),
        out_shape=jax.ShapeDtypeStruct((ndev * ntab, per, embed), jnp.bfloat16),
        scratch_shapes=[
            pltpu.VMEM((ndev, ntab, per, embed), jnp.bfloat16),
            pltpu.SemaphoreType.DMA,
            pltpu.SemaphoreType.DMA,
            pltpu.SemaphoreType.DMA,
        ],
        compiler_params=pltpu.CompilerParams(
            vmem_limit_bytes=48 << 20, collective_id=0, has_side_effects=True
        ),
        name="pool",
    )(ids, lengths.reshape(ntab, 1, samples), tables)


def group_masks(samples):
    n = GROUP * BLK * samples
    r = lax.broadcasted_iota(jnp.int32, (n, n), 0)
    c = lax.broadcasted_iota(jnp.int32, (n, n), 1)
    per = BLK * samples
    same = (r // per == c // per) & (r % samples == c % samples)
    return same


def select_matrix(samples, transposed):
    rows, cols = GROUP * BLK * samples, GROUP * BLK * BLK
    shape = (cols, rows) if transposed else (rows, cols)
    r = lax.broadcasted_iota(jnp.int32, shape, 1 if transposed else 0)
    c = lax.broadcasted_iota(jnp.int32, shape, 0 if transposed else 1)
    hit = (r // (BLK * samples) == c // (BLK * BLK)) & ((r // samples) % BLK == c % BLK)
    return jnp.where(hit, 1.0, 0.0).astype(jnp.bfloat16)


def own_columns(samples):
    rows, cols = GROUP * BLK * samples, GROUP * BLK * BLK
    r = lax.broadcasted_iota(jnp.int32, (rows, cols), 0)
    c = lax.broadcasted_iota(jnp.int32, (rows, cols), 1)
    return r // samples == c // BLK


def gram_kernel(slot_ref, pair_ref, pooled_ref, inter_ref, fields_ref, sel_ref):
    samples, embed = pooled_ref.shape[1:]
    nblocks = fields_ref.shape[0]
    scale = 1.0 / math.sqrt(embed)

    def gather(c, _):
        rows = [
            pooled_ref[slot_ref[c * BLK + i]].astype(jnp.float32) for i in range(BLK)
        ]
        fields_ref[c] = jnp.concatenate(rows, axis=0).astype(jnp.bfloat16)
        return 0

    lax.fori_loop(0, nblocks, gather, 0, unroll=4)
    same = group_masks(samples)
    own = own_columns(samples)
    sel_ref[...] = select_matrix(samples, False)
    width = GROUP * BLK * BLK
    for q in range(NPAIR // GROUP):
        left = jnp.concatenate(
            [fields_ref[pair_ref[2 * (q * GROUP + p)]] for p in range(GROUP)], axis=0
        )
        right = jnp.concatenate(
            [fields_ref[pair_ref[2 * (q * GROUP + p) + 1]] for p in range(GROUP)], axis=0
        )
        gram = lax.dot_general(
            left, right, (((1,), (1,)), ((), ())), preferred_element_type=jnp.float32
        )
        gram = jnp.where(same, gram * scale, 0.0).astype(jnp.bfloat16)
        spread = jnp.dot(gram, sel_ref[...], preferred_element_type=jnp.float32)
        kept = jnp.where(own, spread, 0.0).reshape(GROUP * BLK, samples, width)
        inter_ref[:, q * width : (q + 1) * width] = jnp.sum(kept, axis=0).astype(jnp.bfloat16)


def gram(pooled_all, field_slot, pair_blocks):
    nfields, samples, embed = pooled_all.shape
    nblocks = nfields // BLK
    inter = NPAIR * BLK * BLK
    width = GROUP * BLK * BLK
    return pl.pallas_call(
        gram_kernel,
        grid=(),
        in_specs=[
            pl.BlockSpec(memory_space=pltpu.SMEM),
            pl.BlockSpec(memory_space=pltpu.SMEM),
            pl.BlockSpec(memory_space=pltpu.VMEM),
        ],
        out_specs=[pl.BlockSpec(memory_space=pltpu.VMEM)] * 2,
        out_shape=[
            jax.ShapeDtypeStruct((samples, inter), jnp.bfloat16),
            jax.ShapeDtypeStruct((nblocks, BLK * samples, embed), jnp.bfloat16),
        ],
        scratch_shapes=[pltpu.VMEM((width, width), jnp.bfloat16)],
        compiler_params=pltpu.CompilerParams(vmem_limit_bytes=48 << 20),
        name="gram",
    )(field_slot, pair_blocks.reshape(-1), pooled_all)


def gram_grad_kernel(slot_ref, pair_ref, dinter_ref, fields_ref, out_ref, total_ref, sel_ref):
    samples, embed = out_ref.shape[1:]
    nblocks = fields_ref.shape[0]
    scale = 1.0 / math.sqrt(embed)
    total_ref[...] = jnp.zeros_like(total_ref)
    same = group_masks(samples)
    own = own_columns(samples)
    sel_ref[...] = select_matrix(samples, True)
    width = GROUP * BLK * BLK
    per = BLK * samples
    for q in range(NPAIR // GROUP):
        first = [pair_ref[2 * (q * GROUP + p)] for p in range(GROUP)]
        second = [pair_ref[2 * (q * GROUP + p) + 1] for p in range(GROUP)]
        left = jnp.concatenate([fields_ref[a] for a in first], axis=0)
        right = jnp.concatenate([fields_ref[b] for b in second], axis=0)
        entry = dinter_ref[:, q * width : (q + 1) * width].astype(jnp.float32)
        spread = jnp.broadcast_to(entry[None], (GROUP * BLK, samples, width))
        spread = jnp.where(own, spread.reshape(per * GROUP, width), 0.0).astype(jnp.bfloat16)
        pair = jnp.dot(spread, sel_ref[...], preferred_element_type=jnp.float32)
        pair = jnp.where(same, pair, 0.0).astype(jnp.bfloat16)
        to_left = jnp.dot(pair, right, preferred_element_type=jnp.float32) * scale
        to_right = (
            lax.dot_general(
                pair, left, (((0,), (0,)), ((), ())), preferred_element_type=jnp.float32
            )
            * scale
        )
        for p in range(GROUP):
            total_ref[first[p]] += to_left[p * per : (p + 1) * per]
            total_ref[second[p]] += to_right[p * per : (p + 1) * per]

    def scatter(c, _):
        rows = total_ref[c]
        for i in range(BLK):
            out_ref[slot_ref[c * BLK + i]] = rows[i * samples : (i + 1) * samples].astype(
                jnp.bfloat16
            )
        return 0

    lax.fori_loop(0, nblocks, scatter, 0, unroll=4)


def gram_grad(dinter, fields, field_slot, pair_blocks):
    nblocks, per, embed = fields.shape
    samples = per // BLK
    width = GROUP * BLK * BLK
    return pl.pallas_call(
        gram_grad_kernel,
        grid=(),
        in_specs=[
            pl.BlockSpec(memory_space=pltpu.SMEM),
            pl.BlockSpec(memory_space=pltpu.SMEM),
            pl.BlockSpec(memory_space=pltpu.VMEM),
            pl.BlockSpec(memory_space=pltpu.VMEM),
        ],
        out_specs=pl.BlockSpec(memory_space=pltpu.VMEM),
        out_shape=jax.ShapeDtypeStruct((nblocks * BLK, samples, embed), jnp.bfloat16),
        scratch_shapes=[
            pltpu.VMEM((nblocks, per, embed), jnp.float32),
            pltpu.VMEM((width, width), jnp.bfloat16),
        ],
        compiler_params=pltpu.CompilerParams(vmem_limit_bytes=48 << 20),
        name="gram_grad",
    )(field_slot, pair_blocks.reshape(-1), dinter, fields)


STEP = 512


def dense_kernel(
    inter_ref,
    w_ref,
    b_ref,
    cot_ref,
    over_ref,
    dinter_ref,
    gw_ref,
    gb_ref,
    gath,
    part,
    xrecv,
    sa,
    brecv,
    sb,
    crecv,
    gsend,
    grecv,
    bias,
    ag1_s,
    ag1_r,
    ag2_s,
    ag2_r,
    ag3_s,
    ag3_r,
    rs1_s,
    rs1_r,
    rs2_s,
    rs2_r,
    rs3_s,
    rs3_r,
    z_s,
    z_r,
    zb_s,
    zb_r,
):
    nhalf, ny, nx, ncore, per, width = gath.shape
    nrep = gsend.shape[0]
    samples = ny * nx * ncore * per
    hidden = w_ref.shape[1]
    rep, emb = lax.axis_index("rep"), lax.axis_index("emb")
    y, x, c = emb // (nx * ncore), lax.rem(emb // ncore, nx), lax.rem(emb, ncore)

    def at(yy, xx, cc):
        return (rep, (yy * nx + xx) * ncore + cc)

    xs = [lax.rem(x + k, nx) for k in range(nx)]
    ys = [lax.rem(y + k, ny) for k in range(ny)]
    zs = [lax.rem(rep + k, nrep) for k in range(nrep)]
    mate = at(y, x, 1 - c)
    greet([at(y, xs[k], c) for k in range(1, nx)])
    greet([at(ys[k], x, c) for k in range(1, ny)])
    greet([(zs[k], emb) for k in range(1, nrep)])
    greet([mate])
    for half in range(nhalf):
        gath[half, y, x, c] = inter_ref[:, half * width : (half + 1) * width]
    pl.semaphore_wait(pltpu.get_barrier_semaphore(), nx + ny + nrep - 3 + 1)

    sent = []

    def send(src, dst, send_sem, recv_sem, device):
        copy = remote(src, dst, send_sem, recv_sem, device)
        copy.start()
        sent.append(copy)

    own = [gath.at[half, y, x, c] for half in range(nhalf)]
    for k in range(1, nx):
        send(own[0], own[0], ag1_s.at[0, k], ag1_r.at[0, k], at(y, xs[k], c))
        send(own[1], own[1], ag1_s.at[1, k], ag1_r.at[1, k], at(ys[k], x, c))
    lines = [gath.at[0, y, :, c], gath.at[1, :, x, c]]
    for half in range(nhalf):
        for k in range(1, nx):
            remote(own[half], own[half], ag1_s.at[half, k], ag1_r.at[half, k], mate).wait_recv()
        for k in range(1, nx):
            device = at(ys[k], x, c) if half == 0 else at(y, xs[k], c)
            send(lines[half], lines[half], ag2_s.at[half, k], ag2_r.at[half, k], device)
        send(lines[half], lines[half], ag3_s.at[half, 0], ag3_r.at[half, 0], mate)
    for k in range(1, nx):
        for half in range(nhalf):
            remote(lines[half], lines[half], ag2_s.at[half, k], ag2_r.at[half, k], mate).wait_recv()
            line = gath.at[0, ys[ny - k], :, c] if half == 0 else gath.at[1, :, xs[nx - k], c]
            send(line, line, ag3_s.at[half, k], ag3_r.at[half, k], mate)
    for k in range(nx):
        for half in range(nhalf):
            remote(lines[half], lines[half], ag3_s.at[half, k], ag3_r.at[half, k], mate).wait_recv()

    steps = width // STEP
    pre = jnp.zeros((samples, hidden), jnp.float32)
    for half in range(nhalf):

        def forward(j, total):
            cols = pl.ds(pl.multiple_of(j * STEP, STEP), STEP)
            rows = pl.ds(pl.multiple_of(half * width + j * STEP, STEP), STEP)
            block = gath[half, :, :, :, :, cols].reshape(samples, STEP)
            return total + jnp.dot(block, w_ref[rows], preferred_element_type=jnp.float32)

        pre = lax.fori_loop(0, steps, forward, pre)
    pre = pre + b_ref[...].astype(jnp.float32)
    sig = jax.nn.sigmoid(pre)
    over_ref[...] = (pre * sig).astype(jnp.bfloat16)
    dpre = (cot_ref[...].astype(jnp.float32) * sig * (1.0 + pre * (1.0 - sig))).astype(jnp.bfloat16)

    for half in range(nhalf):

        def backward(j, _):
            cols = pl.ds(pl.multiple_of(j * STEP, STEP), STEP)
            rows = pl.ds(pl.multiple_of(half * width + j * STEP, STEP), STEP)
            block = lax.dot_general(
                dpre, w_ref[rows], (((1,), (1,)), ((), ())), preferred_element_type=jnp.float32
            )
            block = block.reshape(ny, nx, ncore, per, STEP)
            for core in range(ncore):
                part[half, core, :, :, :, cols] = block[:, :, core].astype(jnp.bfloat16)
            return 0

        lax.fori_loop(0, steps, backward, 0)
        send(part.at[half, 1 - c], xrecv.at[half], rs1_s.at[half], rs1_r.at[half], mate)

    gb = jnp.sum(dpre.astype(jnp.float32), axis=0, keepdims=True)
    bias[rep] = jnp.broadcast_to(gb, bias.shape[1:])
    for k in range(1, nrep):
        send(bias.at[rep], bias.at[rep], zb_s.at[k], zb_r.at[k], (zs[k], emb))
    quarter = gsend.shape[1]
    for half in range(nhalf):

        def weights(j, _):
            cols = pl.ds(pl.multiple_of(j * STEP, STEP), STEP)
            block = gath[half, :, :, :, :, cols].reshape(samples, STEP)
            product = lax.dot_general(
                block, dpre, (((0,), (0,)), ((), ())), preferred_element_type=jnp.float32
            )
            place = half * (width // STEP) + j
            per_quarter = quarter // STEP
            rows = pl.ds(pl.multiple_of(lax.rem(place, per_quarter) * STEP, STEP), STEP)
            gsend[place // per_quarter, rows] = product.astype(jnp.bfloat16)
            return 0

        lax.fori_loop(0, steps, weights, 0)
    for k in range(1, nrep):
        send(gsend.at[zs[k]], grecv.at[k - 1], z_s.at[k], z_r.at[k], (zs[k], emb))

    for half in range(nhalf):
        remote(xrecv.at[half], xrecv.at[half], rs1_s.at[half], rs1_r.at[half], mate).wait_recv()

        def add(j, _):
            sa[half, j] = (
                part[half, c, j].astype(jnp.float32) + xrecv[half, j].astype(jnp.float32)
            ).astype(jnp.bfloat16)
            return 0

        lax.fori_loop(0, ny, add, 0)
        for k in range(1, nx):
            if half == 0:
                src, device = sa.at[0, ys[k]], at(ys[k], x, c)
            else:
                src, device = sa.at[1, :, xs[k]], at(y, xs[k], c)
            send(src, brecv.at[half, k - 1], rs2_s.at[half, k], rs2_r.at[half, k], device)
    for half in range(nhalf):
        mine = sa[0, y] if half == 0 else sa[1, :, x]
        total = mine.astype(jnp.float32)
        for k in range(1, nx):
            slot = brecv.at[half, k - 1]
            remote(slot, slot, rs2_s.at[half, k], rs2_r.at[half, k], mate).wait_recv()
            total = total + brecv[half, k - 1].astype(jnp.float32)
        sb[half] = total.astype(jnp.bfloat16)
        for k in range(1, nx):
            place = xs[k] if half == 0 else ys[k]
            device = at(y, xs[k], c) if half == 0 else at(ys[k], x, c)
            send(
                sb.at[half, place],
                crecv.at[half, k - 1],
                rs3_s.at[half, k],
                rs3_r.at[half, k],
                device,
            )
    for half in range(nhalf):
        total = sb[half, x if half == 0 else y].astype(jnp.float32)
        for k in range(1, nx):
            slot = crecv.at[half, k - 1]
            remote(slot, slot, rs3_s.at[half, k], rs3_r.at[half, k], mate).wait_recv()
            total = total + crecv[half, k - 1].astype(jnp.float32)
        dinter_ref[:, half * width : (half + 1) * width] = total.astype(jnp.bfloat16)

    for k in range(1, nrep):
        slot = grecv.at[k - 1]
        remote(slot, slot, z_s.at[k], z_r.at[k], mate).wait_recv()
        remote(bias.at[rep], bias.at[rep], zb_s.at[k], zb_r.at[k], mate).wait_recv()
    total = gsend[rep].astype(jnp.float32)
    for k in range(1, nrep):
        total = total + grecv[k - 1].astype(jnp.float32)
    gw_ref[...] = total.astype(jnp.bfloat16)
    gb_ref[...] = jnp.sum(bias[...], axis=0)[:1]
    for copy in sent:
        copy.wait_send()


def dense(inter, w, b, cot, grid):
    nrep, ny, nx, ncore = grid
    per, features = inter.shape
    samples, hidden = cot.shape
    nhalf, width, quarter = 2, features // 2, features // nrep
    half_rows = (nhalf, ny, nx, per, width)
    dma = pltpu.SemaphoreType.DMA
    bf16 = jnp.bfloat16
    return pl.pallas_call(
        dense_kernel,
        in_specs=[pl.BlockSpec(memory_space=pltpu.VMEM)] * 4,
        out_specs=[pl.BlockSpec(memory_space=pltpu.VMEM)] * 4,
        out_shape=[
            jax.ShapeDtypeStruct((samples, hidden), bf16),
            jax.ShapeDtypeStruct((per, features), bf16),
            jax.ShapeDtypeStruct((quarter, hidden), bf16),
            jax.ShapeDtypeStruct((1, hidden), jnp.float32),
        ],
        scratch_shapes=[
            pltpu.VMEM((nhalf, ny, nx, ncore, per, width), bf16),
            pltpu.VMEM((nhalf, ncore, ny, nx, per, width), bf16),
            pltpu.VMEM(half_rows, bf16),
            pltpu.VMEM(half_rows, bf16),
            pltpu.VMEM((nhalf, nx - 1, nx, per, width), bf16),
            pltpu.VMEM((nhalf, nx, per, width), bf16),
            pltpu.VMEM((nhalf, nx - 1, per, width), bf16),
            pltpu.VMEM((nrep, quarter, hidden), bf16),
            pltpu.VMEM((nrep - 1, quarter, hidden), bf16),
            pltpu.VMEM((nrep, 8, hidden), jnp.float32),
        ]
        + [dma((nhalf, nx))] * 6
        + [dma((nhalf,))] * 2
        + [dma((nhalf, nx))] * 4
        + [dma((nrep,))] * 4,
        compiler_params=pltpu.CompilerParams(
            vmem_limit_bytes=48 << 20, collective_id=1, has_side_effects=True
        ),
        name="dense",
    )(inter, w, b.reshape(1, hidden), cot)


def back_kernel(rows_ref, gw_ref, out_ref, gall_ref, send_sem, recv_sem, own_sem, z_s, z_r):
    ndev = rows_ref.shape[0]
    nrep = gall_ref.shape[0]
    rep, me = lax.axis_index("rep"), lax.axis_index("emb")
    greet_axis(rep, me, ndev)
    peers = [lax.rem(rep + k, nrep) for k in range(nrep)]
    greet([(peers[k], me) for k in range(1, nrep)])
    pl.semaphore_wait(pltpu.get_barrier_semaphore(), ndev - 1 + nrep - 1)

    def send(k, _):
        peer = lax.rem(me + k, ndev)
        remote(rows_ref.at[peer], out_ref.at[me], send_sem, recv_sem, (rep, peer)).start()
        return 0

    lax.fori_loop(1, ndev, send, 0)
    copies = [
        remote(gw_ref, gall_ref.at[rep], z_s.at[k], z_r.at[k], (peers[k], me))
        for k in range(1, nrep)
    ]
    for copy in copies:
        copy.start()
    own = pltpu.make_async_copy(rows_ref.at[me], out_ref.at[me], own_sem.at[0])
    own.start()
    own_gw = pltpu.make_async_copy(gw_ref, gall_ref.at[rep], own_sem.at[1])
    own_gw.start()
    own.wait()
    own_gw.wait()
    for copy in copies:
        copy.wait_recv()
    others = out_ref.at[pl.ds(0, ndev - 1)]
    both = remote(others, others, send_sem, recv_sem, (rep, lax.rem(me + 1, ndev)))
    both.wait_recv()
    both.wait_send()
    for copy in copies:
        copy.wait_send()


def back(rows, gw, nrep):
    dma = pltpu.SemaphoreType.DMA
    return pl.pallas_call(
        back_kernel,
        in_specs=[pl.BlockSpec(memory_space=pltpu.VMEM)] * 2,
        out_specs=[pl.BlockSpec(memory_space=pltpu.VMEM)] * 2,
        out_shape=[
            jax.ShapeDtypeStruct(rows.shape, rows.dtype),
            jax.ShapeDtypeStruct((nrep, *gw.shape), gw.dtype),
        ],
        scratch_shapes=[dma, dma, dma((2,)), dma((nrep,)), dma((nrep,))],
        compiler_params=pltpu.CompilerParams(
            vmem_limit_bytes=48 << 20, collective_id=2, has_side_effects=True
        ),
        name="back",
    )(rows, gw)


def on_device(tables, bag_ids, bag_lengths, field_slot, pair_blocks, w_over, b_over, cotangent):
    ndev, nrep = lax.axis_size("emb"), lax.axis_size("rep")
    ntab, samples_rep, embed = tables.shape[0], bag_ids.shape[1], tables.shape[2]
    samples = samples_rep // ndev
    pooled_all = pool(jnp.swapaxes(bag_ids, 1, 2), bag_lengths, tables, ndev)
    inter, fields = gram(pooled_all, field_slot, pair_blocks)
    over_out, dinter, gw, gb = dense(inter, w_over, b_over, cotangent, (nrep, 4, 4, 2))
    dslots = gram_grad(dinter, fields, field_slot, pair_blocks)
    rows, gw_all = back(dslots.reshape(ndev, ntab, samples, embed), gw, nrep)
    pooled_grad = jnp.swapaxes(rows, 0, 1).reshape(ntab, samples_rep, embed)
    grad_w = gw_all.reshape(w_over.shape).astype(jnp.float32)
    return (over_out, grad_w, gb.reshape(b_over.shape), pooled_grad)


def solution(mesh):
    in_specs = (
        P("emb", None, None),
        P("emb", "rep", None),
        P("emb", "rep"),
        P(),
        P(),
        P(None, "emb"),
        P("emb"),
        P("rep", "emb"),
    )
    out_specs = (P("rep", "emb"), P(None, "emb"), P("emb"), P("emb", "rep", None))
    return jax.shard_map(
        on_device, mesh=mesh, in_specs=in_specs, out_specs=out_specs, check_vma=False
    )
```

```python
import functools
import math

import jax
import jax.numpy as jnp
from jax import lax
from jax.experimental import pallas as pl
from jax.experimental.pallas import tpu as pltpu
from jax.sharding import PartitionSpec as P

BLK = 8
NPAIR = 64
GROUP = 4
WORDS = 176
BITS = 5


MESH = pl.DeviceIdType.MESH
CHUNK = 5


def remote(src, dst, send_sem, recv_sem, device):
    return pltpu.make_async_remote_copy(
        src_ref=src,
        dst_ref=dst,
        send_sem=send_sem,
        recv_sem=recv_sem,
        device_id=device,
        device_id_type=MESH,
    )


def greet(devices):
    barrier = pltpu.get_barrier_semaphore()
    for device in devices:
        pl.semaphore_signal(barrier, inc=1, device_id=device, device_id_type=MESH)


def peer_order(ny, nx, ncore):
    left = [
        (dy, dx, dc)
        for dy in range(ny)
        for dx in range(nx)
        for dc in range(ncore)
        if (dy, dx, dc) != (0, 0, 0)
    ]

    def links(offset):
        used = []
        for axis, (step, size) in enumerate(((offset[0], ny), (offset[1], nx))):
            if 0 < step <= size // 2:
                used.append(2 * axis)
            if step >= size - size // 2 and step > 0:
                used.append(2 * axis + 1)
        return used

    order, load = [], [0] * 4

    def cost(offset):
        after = list(load)
        for link in links(offset):
            after[link] += 1
        return max(after) - min(after)

    while left:
        best = min(left, key=cost)
        left.remove(best)
        order.append(best)
        for link in links(best):
            load[link] += 1
    return order


def pooled_rows(ids, lengths, table):
    bag, samples = ids.shape
    rows, embed = table.shape
    used = lax.broadcasted_iota(jnp.int32, (bag, samples), 0) < lengths
    field = ids // WORDS
    word = ids - field * WORDS
    value = jnp.where(used, jnp.left_shift(1, field * BITS), 0)
    halves = []
    for half in range(samples // 128):
        lanes = slice(half * 128, half * 128 + 128)
        row = lax.broadcasted_iota(jnp.int32, (WORDS, 128), 0)
        total = jnp.zeros((WORDS, 128), jnp.int32)
        for k in range(bag):
            total += jnp.where(row == word[k : k + 1, lanes], value[k : k + 1, lanes], 0)
        halves.append(total)
    counts = jnp.concatenate(halves, axis=1)
    chunks = []
    for part, start in enumerate(range(0, rows, WORDS)):
        chunk = (counts[: min(WORDS, rows - start)] >> (BITS * part)) & ((1 << BITS) - 1)
        chunks.append(chunk.astype(jnp.float32).astype(jnp.bfloat16))
    pooled = lax.dot_general(
        table,
        jnp.concatenate(chunks, axis=0),
        (((0,), (0,)), ((), ())),
        preferred_element_type=jnp.float32,
    )
    return pooled.T.astype(jnp.bfloat16)


def group_masks(samples):
    n = GROUP * BLK * samples
    r = lax.broadcasted_iota(jnp.int32, (n, n), 0)
    c = lax.broadcasted_iota(jnp.int32, (n, n), 1)
    per = BLK * samples
    same = (r // per == c // per) & (r % samples == c % samples)
    return same


def select_matrix(samples, transposed):
    rows, cols = GROUP * BLK * samples, GROUP * BLK * BLK
    shape = (cols, rows) if transposed else (rows, cols)
    r = lax.broadcasted_iota(jnp.int32, shape, 1 if transposed else 0)
    c = lax.broadcasted_iota(jnp.int32, shape, 0 if transposed else 1)
    hit = (r // (BLK * samples) == c // (BLK * BLK)) & ((r // samples) % BLK == c % BLK)
    return jnp.where(hit, 1.0, 0.0).astype(jnp.bfloat16)


def own_columns(samples):
    rows, cols = GROUP * BLK * samples, GROUP * BLK * BLK
    r = lax.broadcasted_iota(jnp.int32, (rows, cols), 0)
    c = lax.broadcasted_iota(jnp.int32, (rows, cols), 1)
    return r // samples == c // BLK


STEP = 512


def forward_kernel(
    slot_ref,
    pair_ref,
    ids_hbm,
    len_ref,
    tables_hbm,
    w_hbm,
    b_ref,
    cot_hbm,
    fields_ref,
    over_ref,
    dinter_ref,
    gw_ref,
    gb_ref,
    ids_ref,
    table_ref,
    rows_ref,
    pooled_ref,
    sel_ref,
    w_ref,
    cot_ref,
    gath,
    part,
    xrecv,
    sa,
    brecv,
    sb,
    crecv,
    gsend,
    grecv,
    bias,
    ag1_s,
    ag1_r,
    ag2_s,
    ag2_r,
    ag3_s,
    ag3_r,
    rs1_s,
    rs1_r,
    rs2_s,
    rs2_r,
    rs3_s,
    rs3_r,
    z_s,
    z_r,
    zb_s,
    zb_r,
    own_sem,
    table_sem,
    a2a_s,
    a2a_r,
):
    nhalf, ny, nx, ncore, per, width = gath.shape
    nrep = gsend.shape[0]
    samples = ny * nx * ncore * per
    hidden = w_ref.shape[1]
    rep, emb = lax.axis_index("rep"), lax.axis_index("emb")
    y, x, c = emb // (nx * ncore), lax.rem(emb // ncore, nx), lax.rem(emb, ncore)

    def at(yy, xx, cc):
        return (rep, (yy * nx + xx) * ncore + cc)

    xs = [lax.rem(x + k, nx) for k in range(nx)]
    ys = [lax.rem(y + k, ny) for k in range(ny)]
    zs = [lax.rem(rep + k, nrep) for k in range(nrep)]
    mate = at(y, x, 1 - c)
    peers = [
        at(ys[dy], xs[dx], lax.rem(c + dc, ncore)) for dy, dx, dc in peer_order(ny, nx, ncore)
    ]
    ndev, ntab, _, embed = rows_ref.shape
    nblocks = fields_ref.shape[0]

    get_ids = pltpu.make_async_copy(ids_hbm, ids_ref, own_sem.at[0])
    get_ids.start()

    def get_tables(step):
        slot = lax.rem(step, 2)
        return pltpu.make_async_copy(
            tables_hbm.at[pl.ds(step * CHUNK, CHUNK)], table_ref.at[slot], table_sem.at[slot]
        )

    get_tables(0).start()
    get_w = pltpu.make_async_copy(w_hbm, w_ref, own_sem.at[1])
    get_w.start()
    get_cot = pltpu.make_async_copy(cot_hbm, cot_ref, own_sem.at[2])
    get_cot.start()
    greet(peers)
    greet([(zs[k], emb) for k in range(1, nrep)])
    get_ids.wait()

    def pool_step(step, _):
        slot = lax.rem(step, 2)
        get_tables(step).wait()

        @pl.when(step + 1 < ntab // CHUNK)
        def _():
            get_tables(step + 1).start()

        start = step * CHUNK
        for t in range(CHUNK):
            rows = pooled_rows(ids_ref[start + t], len_ref[pl.ds(start + t, 1)], table_ref[slot, t])
            rows_ref[:, start + t] = rows.reshape(ndev, per, embed)

        @pl.when(step == 0)
        def _():
            pl.semaphore_wait(pltpu.get_barrier_semaphore(), ndev - 1 + nrep - 1)

        for _, peer in peers:
            remote(
                rows_ref.at[peer, pl.ds(start, CHUNK)],
                pooled_ref.at[pl.ds(emb * ntab + start, CHUNK)],
                a2a_s,
                a2a_r,
                (rep, peer),
            ).start()
        return 0

    lax.fori_loop(0, ntab // CHUNK, pool_step, 0)
    own_rows = pltpu.make_async_copy(
        rows_ref.at[emb], pooled_ref.at[pl.ds(emb * ntab, ntab)], own_sem.at[3]
    )
    own_rows.start()
    same = group_masks(per)
    own_cols = own_columns(per)
    sel_ref[...] = select_matrix(per, False)
    own_rows.wait()
    others = pooled_ref.at[pl.ds(0, (ndev - 1) * ntab)]
    remote(others, others, a2a_s, a2a_r, mate).wait_recv()

    def gather(block, _):
        rows = [
            pooled_ref[slot_ref[block * BLK + i]].astype(jnp.float32) for i in range(BLK)
        ]
        fields_ref[block] = jnp.concatenate(rows, axis=0).astype(jnp.bfloat16)
        return 0

    lax.fori_loop(0, nblocks, gather, 0, unroll=4)

    sent = []

    def send(src, dst, send_sem, recv_sem, device):
        copy = remote(src, dst, send_sem, recv_sem, device)
        copy.start()
        sent.append(copy)

    scale = 1.0 / math.sqrt(embed)
    group = GROUP * BLK * BLK
    own = [gath.at[half, y, x, c] for half in range(nhalf)]
    for half in range(nhalf):
        for q in range(width // group):
            first = half * (NPAIR // nhalf) + q * GROUP
            left = jnp.concatenate(
                [fields_ref[pair_ref[0, first + p]] for p in range(GROUP)], axis=0
            )
            right = jnp.concatenate(
                [fields_ref[pair_ref[1, first + p]] for p in range(GROUP)], axis=0
            )
            gram = lax.dot_general(
                left, right, (((1,), (1,)), ((), ())), preferred_element_type=jnp.float32
            )
            gram = jnp.where(same, gram * scale, 0.0).astype(jnp.bfloat16)
            spread = jnp.dot(gram, sel_ref[...], preferred_element_type=jnp.float32)
            kept = jnp.where(own_cols, spread, 0.0).reshape(GROUP * BLK, per, group)
            gath[half, y, x, c, :, q * group : (q + 1) * group] = jnp.sum(kept, axis=0).astype(
                jnp.bfloat16
            )
        for k in range(1, nx):
            device = at(y, xs[k], c) if half == 0 else at(ys[k], x, c)
            send(own[half], own[half], ag1_s.at[half, k], ag1_r.at[half, k], device)
    lines = [gath.at[0, y, :, c], gath.at[1, :, x, c]]
    for half in range(nhalf):
        for k in range(1, nx):
            remote(own[half], own[half], ag1_s.at[half, k], ag1_r.at[half, k], mate).wait_recv()
        for k in range(1, nx):
            device = at(ys[k], x, c) if half == 0 else at(y, xs[k], c)
            send(lines[half], lines[half], ag2_s.at[half, k], ag2_r.at[half, k], device)
        send(lines[half], lines[half], ag3_s.at[half, 0], ag3_r.at[half, 0], mate)
    for k in range(1, nx):
        for half in range(nhalf):
            remote(lines[half], lines[half], ag2_s.at[half, k], ag2_r.at[half, k], mate).wait_recv()
            line = gath.at[0, ys[ny - k], :, c] if half == 0 else gath.at[1, :, xs[nx - k], c]
            send(line, line, ag3_s.at[half, k], ag3_r.at[half, k], mate)
    for k in range(nx):
        for half in range(nhalf):
            remote(lines[half], lines[half], ag3_s.at[half, k], ag3_r.at[half, k], mate).wait_recv()

    get_w.wait()
    get_cot.wait()
    steps = width // STEP
    pre = jnp.zeros((samples, hidden), jnp.float32)
    for half in range(nhalf):

        def forward(j, total):
            cols = pl.ds(pl.multiple_of(j * STEP, STEP), STEP)
            rows = pl.ds(pl.multiple_of(half * width + j * STEP, STEP), STEP)
            block = gath[half, :, :, :, :, cols].reshape(samples, STEP)
            return total + jnp.dot(block, w_ref[rows], preferred_element_type=jnp.float32)

        pre = lax.fori_loop(0, steps, forward, pre)
    pre = pre + b_ref[...].astype(jnp.float32)
    sig = jax.nn.sigmoid(pre)
    over_ref[...] = (pre * sig).astype(jnp.bfloat16)
    dpre = (cot_ref[...].astype(jnp.float32) * sig * (1.0 + pre * (1.0 - sig))).astype(jnp.bfloat16)

    for half in range(nhalf):

        def backward(j, _):
            cols = pl.ds(pl.multiple_of(j * STEP, STEP), STEP)
            rows = pl.ds(pl.multiple_of(half * width + j * STEP, STEP), STEP)
            block = lax.dot_general(
                dpre, w_ref[rows], (((1,), (1,)), ((), ())), preferred_element_type=jnp.float32
            )
            block = block.reshape(ny, nx, ncore, per, STEP)
            for core in range(ncore):
                part[half, core, :, :, :, cols] = block[:, :, core].astype(jnp.bfloat16)
            return 0

        lax.fori_loop(0, steps, backward, 0)
        send(part.at[half, 1 - c], xrecv.at[half], rs1_s.at[half], rs1_r.at[half], mate)

    gb = jnp.sum(dpre.astype(jnp.float32), axis=0, keepdims=True)
    bias[rep] = jnp.broadcast_to(gb, bias.shape[1:])
    for k in range(1, nrep):
        send(bias.at[rep], bias.at[rep], zb_s.at[k], zb_r.at[k], (zs[k], emb))
    quarter = gsend.shape[1]
    for half in range(nhalf):

        def weights(j, _):
            cols = pl.ds(pl.multiple_of(j * STEP, STEP), STEP)
            block = gath[half, :, :, :, :, cols].reshape(samples, STEP)
            product = lax.dot_general(
                block, dpre, (((0,), (0,)), ((), ())), preferred_element_type=jnp.float32
            )
            place = half * (width // STEP) + j
            per_quarter = quarter // STEP
            rows = pl.ds(pl.multiple_of(lax.rem(place, per_quarter) * STEP, STEP), STEP)
            gsend[place // per_quarter, rows] = product.astype(jnp.bfloat16)
            return 0

        lax.fori_loop(0, steps, weights, 0)
    for k in range(1, nrep):
        send(gsend.at[zs[k]], grecv.at[k - 1], z_s.at[k], z_r.at[k], (zs[k], emb))

    for half in range(nhalf):
        remote(xrecv.at[half], xrecv.at[half], rs1_s.at[half], rs1_r.at[half], mate).wait_recv()

        def add(j, _):
            sa[half, j] = (
                part[half, c, j].astype(jnp.float32) + xrecv[half, j].astype(jnp.float32)
            ).astype(jnp.bfloat16)
            return 0

        lax.fori_loop(0, ny, add, 0)
        for k in range(1, nx):
            if half == 0:
                src, device = sa.at[0, ys[k]], at(ys[k], x, c)
            else:
                src, device = sa.at[1, :, xs[k]], at(y, xs[k], c)
            send(src, brecv.at[half, k - 1], rs2_s.at[half, k], rs2_r.at[half, k], device)
    for half in range(nhalf):
        mine = sa[0, y] if half == 0 else sa[1, :, x]
        total = mine.astype(jnp.float32)
        for k in range(1, nx):
            slot = brecv.at[half, k - 1]
            remote(slot, slot, rs2_s.at[half, k], rs2_r.at[half, k], mate).wait_recv()
            total = total + brecv[half, k - 1].astype(jnp.float32)
        sb[half] = total.astype(jnp.bfloat16)
        for k in range(1, nx):
            place = xs[k] if half == 0 else ys[k]
            device = at(y, xs[k], c) if half == 0 else at(ys[k], x, c)
            send(
                sb.at[half, place],
                crecv.at[half, k - 1],
                rs3_s.at[half, k],
                rs3_r.at[half, k],
                device,
            )
    for half in range(nhalf):
        total = sb[half, x if half == 0 else y].astype(jnp.float32)
        for k in range(1, nx):
            slot = crecv.at[half, k - 1]
            remote(slot, slot, rs3_s.at[half, k], rs3_r.at[half, k], mate).wait_recv()
            total = total + crecv[half, k - 1].astype(jnp.float32)
        dinter_ref[:, half * width : (half + 1) * width] = total.astype(jnp.bfloat16)

    for k in range(1, nrep):
        slot = grecv.at[k - 1]
        remote(slot, slot, z_s.at[k], z_r.at[k], mate).wait_recv()
        remote(bias.at[rep], bias.at[rep], zb_s.at[k], zb_r.at[k], mate).wait_recv()
    total = gsend[rep].astype(jnp.float32)
    for k in range(1, nrep):
        total = total + grecv[k - 1].astype(jnp.float32)
    gw_ref[...] = total.astype(jnp.bfloat16)
    gb_ref[...] = jnp.sum(bias[...], axis=0)[:1]
    sources = rows_ref.at[pl.ds(0, ndev - 1)]
    remote(sources, sources, a2a_s, a2a_r, mate).wait_send()
    for copy in sent:
        copy.wait_send()


def forward(ids, lengths, tables, field_slot, pairs, w, b, cot, grid):
    nrep, ny, nx, ncore = grid
    ndev = ny * nx * ncore
    ntab, bag, samples = ids.shape
    rows, embed = tables.shape[1:]
    per = samples // ndev
    features, hidden = w.shape
    nblocks = ndev * ntab // BLK
    nhalf, width, quarter = 2, features // 2, features // nrep
    half_rows = (nhalf, ny, nx, per, width)
    group = GROUP * BLK * BLK
    dma = pltpu.SemaphoreType.DMA
    bf16 = jnp.bfloat16
    smem = pl.BlockSpec(memory_space=pltpu.SMEM)
    vmem = pl.BlockSpec(memory_space=pltpu.VMEM)
    anywhere = pl.BlockSpec(memory_space=pl.ANY)
    return pl.pallas_call(
        forward_kernel,
        in_specs=[smem, smem, anywhere, vmem, anywhere, anywhere, vmem, anywhere],
        out_specs=[vmem] * 5,
        out_shape=[
            jax.ShapeDtypeStruct((nblocks, BLK * per, embed), bf16),
            jax.ShapeDtypeStruct((samples, hidden), bf16),
            jax.ShapeDtypeStruct((per, features), bf16),
            jax.ShapeDtypeStruct((quarter, hidden), bf16),
            jax.ShapeDtypeStruct((1, hidden), jnp.float32),
        ],
        scratch_shapes=[
            pltpu.VMEM((ntab, bag, samples), jnp.int32),
            pltpu.VMEM((2, CHUNK, rows, embed), bf16),
            pltpu.VMEM((ndev, ntab, per, embed), bf16),
            pltpu.VMEM((ndev * ntab, per, embed), bf16),
            pltpu.VMEM((group, group), bf16),
            pltpu.VMEM((features, hidden), bf16),
            pltpu.VMEM((samples, hidden), bf16),
            pltpu.VMEM((nhalf, ny, nx, ncore, per, width), bf16),
            pltpu.VMEM((nhalf, ncore, ny, nx, per, width), bf16),
            pltpu.VMEM(half_rows, bf16),
            pltpu.VMEM(half_rows, bf16),
            pltpu.VMEM((nhalf, nx - 1, nx, per, width), bf16),
            pltpu.VMEM((nhalf, nx, per, width), bf16),
            pltpu.VMEM((nhalf, nx - 1, per, width), bf16),
            pltpu.VMEM((nrep, quarter, hidden), bf16),
            pltpu.VMEM((nrep - 1, quarter, hidden), bf16),
            pltpu.VMEM((nrep, 8, hidden), jnp.float32),
        ]
        + [dma((nhalf, nx))] * 6
        + [dma((nhalf,))] * 2
        + [dma((nhalf, nx))] * 4
        + [dma((nrep,))] * 4
        + [dma((4,)), dma((2,)), dma, dma],
        compiler_params=pltpu.CompilerParams(
            vmem_limit_bytes=60 << 20, collective_id=0, has_side_effects=True
        ),
        name="forward",
    )(
        field_slot,
        pairs,
        ids,
        lengths,
        tables,
        w,
        b.reshape(1, hidden),
        cot,
    )


def gram_grad_kernel(
    slot_ref,
    pair_ref,
    dinter_ref,
    fields_ref,
    over_ref,
    gb_ref,
    out_ref,
    over_out_ref,
    gb_out_ref,
    total_ref,
    sel_ref,
):
    over_out_ref[...] = over_ref[...]
    gb_out_ref[...] = gb_ref[...]
    samples, embed = out_ref.shape[1:]
    nblocks = fields_ref.shape[0]
    scale = 1.0 / math.sqrt(embed)
    total_ref[...] = jnp.zeros_like(total_ref)
    same = group_masks(samples)
    own = own_columns(samples)
    sel_ref[...] = select_matrix(samples, True)
    width = GROUP * BLK * BLK
    per = BLK * samples
    for q in range(NPAIR // GROUP):
        first = [pair_ref[0, q * GROUP + p] for p in range(GROUP)]
        second = [pair_ref[1, q * GROUP + p] for p in range(GROUP)]
        left = jnp.concatenate([fields_ref[a] for a in first], axis=0)
        right = jnp.concatenate([fields_ref[b] for b in second], axis=0)
        entry = dinter_ref[:, q * width : (q + 1) * width].astype(jnp.float32)
        spread = jnp.broadcast_to(entry[None], (GROUP * BLK, samples, width))
        spread = jnp.where(own, spread.reshape(per * GROUP, width), 0.0).astype(jnp.bfloat16)
        pair = jnp.dot(spread, sel_ref[...], preferred_element_type=jnp.float32)
        pair = jnp.where(same, pair, 0.0).astype(jnp.bfloat16)
        to_left = jnp.dot(pair, right, preferred_element_type=jnp.float32) * scale
        to_right = (
            lax.dot_general(
                pair, left, (((0,), (0,)), ((), ())), preferred_element_type=jnp.float32
            )
            * scale
        )
        for p in range(GROUP):
            total_ref[first[p]] += to_left[p * per : (p + 1) * per]
            total_ref[second[p]] += to_right[p * per : (p + 1) * per]

    def scatter(c, _):
        rows = total_ref[c]
        for i in range(BLK):
            out_ref[slot_ref[c * BLK + i]] = rows[i * samples : (i + 1) * samples].astype(
                jnp.bfloat16
            )
        return 0

    lax.fori_loop(0, nblocks, scatter, 0, unroll=4)


def gram_grad(dinter, fields, field_slot, pairs, over, gb):
    nblocks, per, embed = fields.shape
    samples = per // BLK
    width = GROUP * BLK * BLK
    return pl.pallas_call(
        gram_grad_kernel,
        grid=(),
        in_specs=[
            pl.BlockSpec(memory_space=pltpu.SMEM),
            pl.BlockSpec(memory_space=pltpu.SMEM),
        ]
        + [pl.BlockSpec(memory_space=pltpu.VMEM)] * 4,
        out_specs=[pl.BlockSpec(memory_space=pltpu.VMEM)] * 3,
        out_shape=[
            jax.ShapeDtypeStruct((nblocks * BLK, samples, embed), jnp.bfloat16),
            jax.ShapeDtypeStruct(over.shape, over.dtype),
            jax.ShapeDtypeStruct(gb.shape, gb.dtype),
        ],
        scratch_shapes=[
            pltpu.VMEM((nblocks, per, embed), jnp.float32),
            pltpu.VMEM((width, width), jnp.bfloat16),
        ],
        compiler_params=pltpu.CompilerParams(vmem_limit_bytes=48 << 20),
        name="gram_grad",
    )(field_slot, pairs, dinter, fields, over, gb)


def back_kernel(ny, nx, ncore, rows_ref, gw_ref, out_ref, gall_ref, send_sem, recv_sem, own_sem, z_s, z_r):
    ndev = rows_ref.shape[0]
    nrep = gall_ref.shape[0]
    rep, me = lax.axis_index("rep"), lax.axis_index("emb")
    y, x, c = me // (nx * ncore), lax.rem(me // ncore, nx), lax.rem(me, ncore)
    places = [
        (lax.rem(y + dy, ny) * nx + lax.rem(x + dx, nx)) * ncore + lax.rem(c + dc, ncore)
        for dy, dx, dc in peer_order(ny, nx, ncore)
    ]
    greet([(rep, place) for place in places])
    peers = [lax.rem(rep + k, nrep) for k in range(nrep)]
    greet([(peers[k], me) for k in range(1, nrep)])
    pl.semaphore_wait(pltpu.get_barrier_semaphore(), ndev - 1 + nrep - 1)

    for peer in places:
        remote(rows_ref.at[peer], out_ref.at[me], send_sem, recv_sem, (rep, peer)).start()
    copies = [
        remote(gw_ref, gall_ref.at[rep], z_s.at[k], z_r.at[k], (peers[k], me))
        for k in range(1, nrep)
    ]
    for copy in copies:
        copy.start()
    own = pltpu.make_async_copy(rows_ref.at[me], out_ref.at[me], own_sem.at[0])
    own.start()
    own_gw = pltpu.make_async_copy(gw_ref, gall_ref.at[rep], own_sem.at[1])
    own_gw.start()
    own.wait()
    own_gw.wait()
    for copy in copies:
        copy.wait_recv()
    others = out_ref.at[pl.ds(0, ndev - 1)]
    both = remote(others, others, send_sem, recv_sem, (rep, lax.rem(me + 1, ndev)))
    both.wait_recv()
    both.wait_send()
    for copy in copies:
        copy.wait_send()


def back(rows, gw, grid):
    nrep = grid[0]
    dma = pltpu.SemaphoreType.DMA
    return pl.pallas_call(
        functools.partial(back_kernel, *grid[1:]),
        in_specs=[pl.BlockSpec(memory_space=pltpu.VMEM)] * 2,
        out_specs=[pl.BlockSpec(memory_space=pltpu.VMEM)] * 2,
        out_shape=[
            jax.ShapeDtypeStruct(rows.shape, rows.dtype),
            jax.ShapeDtypeStruct((nrep, *gw.shape), gw.dtype),
        ],
        scratch_shapes=[dma, dma, dma((2,)), dma((nrep,)), dma((nrep,))],
        compiler_params=pltpu.CompilerParams(
            vmem_limit_bytes=48 << 20, collective_id=1, has_side_effects=True
        ),
        name="back",
    )(rows, gw)


def on_device(tables, bag_ids, bag_lengths, field_slot, pair_blocks, w_over, b_over, cotangent):
    grid = (lax.axis_size("rep"), 4, 4, 2)
    ndev = lax.axis_size("emb")
    ntab, samples_rep, embed = tables.shape[0], bag_ids.shape[1], tables.shape[2]
    samples = samples_rep // ndev
    ids, pairs = jnp.swapaxes(bag_ids, 1, 2), pair_blocks.T
    fields, over, dinter, gw, gb = forward(
        ids, bag_lengths, tables, field_slot, pairs, w_over, b_over, cotangent, grid
    )
    dslots, over_out, grad_b = gram_grad(dinter, fields, field_slot, pairs, over, gb)
    rows, gw_all = back(dslots.reshape(ndev, ntab, samples, embed), gw, grid)
    pooled_grad = jnp.swapaxes(rows, 0, 1).reshape(ntab, samples_rep, embed)
    grad_w = gw_all.reshape(w_over.shape).astype(jnp.float32)
    return (over_out, grad_w, grad_b.reshape(b_over.shape), pooled_grad)


def solution(mesh):
    in_specs = (
        P("emb", None, None),
        P("emb", "rep", None),
        P("emb", "rep"),
        P(),
        P(),
        P(None, "emb"),
        P("emb"),
        P("rep", "emb"),
    )
    out_specs = (P("rep", "emb"), P(None, "emb"), P("emb"), P("emb", "rep", None))
    return jax.shard_map(
        on_device, mesh=mesh, in_specs=in_specs, out_specs=out_specs, check_vma=False
    )
```

```python
import functools
import math

import jax
import jax.numpy as jnp
from jax import lax
from jax.experimental import pallas as pl
from jax.experimental.pallas import tpu as pltpu
from jax.sharding import PartitionSpec as P

BLK = 8
NPAIR = 64
GROUP = 4
WORDS = 176
BITS = 5


MESH = pl.DeviceIdType.MESH
CHUNK = 5


def remote(src, dst, send_sem, recv_sem, device):
    return pltpu.make_async_remote_copy(
        src_ref=src,
        dst_ref=dst,
        send_sem=send_sem,
        recv_sem=recv_sem,
        device_id=device,
        device_id_type=MESH,
    )


def greet(devices):
    barrier = pltpu.get_barrier_semaphore()
    for device in devices:
        pl.semaphore_signal(barrier, inc=1, device_id=device, device_id_type=MESH)


def peer_order(ny, nx, ncore):
    left = [
        (dy, dx, dc)
        for dy in range(ny)
        for dx in range(nx)
        for dc in range(ncore)
        if (dy, dx, dc) != (0, 0, 0)
    ]

    def links(offset):
        used = []
        for axis, (step, size) in enumerate(((offset[0], ny), (offset[1], nx))):
            if 0 < step <= size // 2:
                used.append(2 * axis)
            if step >= size - size // 2 and step > 0:
                used.append(2 * axis + 1)
        return used

    order, load = [], [0] * 4

    def cost(offset):
        after = list(load)
        for link in links(offset):
            after[link] += 1
        return max(after) - min(after)

    while left:
        best = min(left, key=cost)
        left.remove(best)
        order.append(best)
        for link in links(best):
            load[link] += 1
    return order


def pooled_rows(ids, lengths, table):
    bag, samples = ids.shape
    rows, embed = table.shape
    used = lax.broadcasted_iota(jnp.int32, (bag, samples), 0) < lengths
    field = ids // WORDS
    word = ids - field * WORDS
    value = jnp.where(used, jnp.left_shift(1, field * BITS), 0)
    halves = []
    for half in range(samples // 128):
        lanes = slice(half * 128, half * 128 + 128)
        row = lax.broadcasted_iota(jnp.int32, (WORDS, 128), 0)
        total = jnp.zeros((WORDS, 128), jnp.int32)
        for k in range(bag):
            total += jnp.where(row == word[k : k + 1, lanes], value[k : k + 1, lanes], 0)
        halves.append(total)
    counts = jnp.concatenate(halves, axis=1)
    chunks = []
    for part, start in enumerate(range(0, rows, WORDS)):
        chunk = (counts[: min(WORDS, rows - start)] >> (BITS * part)) & ((1 << BITS) - 1)
        chunks.append(chunk.astype(jnp.float32).astype(jnp.bfloat16))
    pooled = lax.dot_general(
        table,
        jnp.concatenate(chunks, axis=0),
        (((0,), (0,)), ((), ())),
        preferred_element_type=jnp.float32,
    )
    return pooled.T.astype(jnp.bfloat16)


def group_masks(samples):
    n = GROUP * BLK * samples
    r = lax.broadcasted_iota(jnp.int32, (n, n), 0)
    c = lax.broadcasted_iota(jnp.int32, (n, n), 1)
    per = BLK * samples
    same = (r // per == c // per) & (r % samples == c % samples)
    return same


def select_matrix(samples, transposed):
    rows, cols = GROUP * BLK * samples, GROUP * BLK * BLK
    shape = (cols, rows) if transposed else (rows, cols)
    r = lax.broadcasted_iota(jnp.int32, shape, 1 if transposed else 0)
    c = lax.broadcasted_iota(jnp.int32, shape, 0 if transposed else 1)
    hit = (r // (BLK * samples) == c // (BLK * BLK)) & ((r // samples) % BLK == c % BLK)
    return jnp.where(hit, 1.0, 0.0).astype(jnp.bfloat16)


def own_columns(samples):
    rows, cols = GROUP * BLK * samples, GROUP * BLK * BLK
    r = lax.broadcasted_iota(jnp.int32, (rows, cols), 0)
    c = lax.broadcasted_iota(jnp.int32, (rows, cols), 1)
    return r // samples == c // BLK


STEP = 512


def scatter_index(pair_rows, slots):
    entries, nfields = 2 * pair_rows.shape[1], slots.shape[1]
    block = jnp.concatenate([pair_rows[0:1], pair_rows[1:2]], axis=1)
    square = (entries, entries)
    down = lax.broadcasted_iota(jnp.int32, square, 0)
    across = lax.broadcasted_iota(jnp.int32, square, 1)
    of_col = jnp.broadcast_to(block, square)
    of_row = of_col.T
    earlier = (of_row == of_col) & (down < across)
    rank = jnp.sum(jnp.where((of_row < of_col) | earlier, 1, 0), axis=0, keepdims=True)
    repeat = jnp.sum(jnp.where(earlier, 1, 0), axis=0, keepdims=True)
    hit = jnp.broadcast_to(rank, square).T == across
    order = jnp.sum(jnp.where(hit, down, 0), axis=0, keepdims=True)
    again = jnp.sum(jnp.where(hit, jnp.broadcast_to(repeat, square).T, 0), axis=0, keepdims=True)

    wide = (entries, nfields)
    own_block = lax.broadcasted_iota(jnp.int32, wide, 1) // BLK
    upto = jnp.where(of_row[:, :1] <= own_block, 1, 0)
    last = jnp.sum(upto, axis=0, keepdims=True) - 1
    piece = last * BLK + lax.broadcasted_iota(jnp.int32, (1, nfields), 1) % BLK
    places = []
    for start in range(0, nfields, entries):
        slot = lax.broadcasted_iota(jnp.int32, wide, 0) + start
        found = jnp.sum(jnp.where(slot == slots, piece, 0), axis=1, keepdims=True)
        row = jnp.broadcast_to(found, square).T
        places.append(jnp.clip(row[0:1], 0, entries * BLK - 1))
    return jnp.clip(order, 0, entries - 1), again, places


def step_kernel(
    slot_hbm,
    pair_hbm,
    ids_hbm,
    len_ref,
    tables_hbm,
    w_hbm,
    b_ref,
    cot_hbm,
    over_ref,
    gb_ref,
    out_ref,
    gall_ref,
    slot_ref,
    pair_ref,
    slot_row,
    pair_rows,
    index_rows,
    index_ref,
    fields_ref,
    dinter_ref,
    gw_ref,
    contrib,
    total_ref,
    back_ref,
    ids_ref,
    table_ref,
    rows_ref,
    pooled_ref,
    sel_ref,
    sel_t_ref,
    w_ref,
    cot_ref,
    gath,
    part,
    xrecv,
    sa,
    brecv,
    sb,
    crecv,
    gsend,
    grecv,
    bias,
    ag1_s,
    ag1_r,
    ag2_s,
    ag2_r,
    ag3_s,
    ag3_r,
    rs1_s,
    rs1_r,
    rs2_s,
    rs2_r,
    rs3_s,
    rs3_r,
    z_s,
    z_r,
    zb_s,
    zb_r,
    own_sem,
    table_sem,
    a2a_s,
    a2a_r,
    back_s,
    back_r,
    za_s,
    za_r,
):
    nhalf, ny, nx, ncore, per, width = gath.shape
    nrep = gsend.shape[0]
    samples = ny * nx * ncore * per
    hidden = w_ref.shape[1]
    rep, emb = lax.axis_index("rep"), lax.axis_index("emb")
    y, x, c = emb // (nx * ncore), lax.rem(emb // ncore, nx), lax.rem(emb, ncore)

    def at(yy, xx, cc):
        return (rep, (yy * nx + xx) * ncore + cc)

    xs = [lax.rem(x + k, nx) for k in range(nx)]
    ys = [lax.rem(y + k, ny) for k in range(ny)]
    zs = [lax.rem(rep + k, nrep) for k in range(nrep)]
    mate = at(y, x, 1 - c)
    peers = [
        at(ys[dy], xs[dx], lax.rem(c + dc, ncore)) for dy, dx, dc in peer_order(ny, nx, ncore)
    ]
    ndev, ntab, _, embed = rows_ref.shape
    nblocks = fields_ref.shape[0]

    get_ids = pltpu.make_async_copy(ids_hbm, ids_ref, own_sem.at[0])
    get_ids.start()
    small = [
        pltpu.make_async_copy(slot_hbm, slot_ref, own_sem.at[4]),
        pltpu.make_async_copy(pair_hbm, pair_ref, own_sem.at[5]),
        pltpu.make_async_copy(slot_hbm, slot_row.at[0], own_sem.at[6]),
        pltpu.make_async_copy(pair_hbm, pair_rows, own_sem.at[7]),
    ]
    for copy in small:
        copy.start()

    def get_tables(step):
        slot = lax.rem(step, 2)
        return pltpu.make_async_copy(
            tables_hbm.at[pl.ds(step * CHUNK, CHUNK)], table_ref.at[slot], table_sem.at[slot]
        )

    get_tables(0).start()
    get_w = pltpu.make_async_copy(w_hbm, w_ref, own_sem.at[1])
    get_w.start()
    get_cot = pltpu.make_async_copy(cot_hbm, cot_ref, own_sem.at[2])
    get_cot.start()
    greet(peers)
    greet([(zs[k], emb) for k in range(1, nrep)])
    get_ids.wait()

    def pool_step(step, _):
        slot = lax.rem(step, 2)
        get_tables(step).wait()

        @pl.when(step + 1 < ntab // CHUNK)
        def _():
            get_tables(step + 1).start()

        start = step * CHUNK
        for t in range(CHUNK):
            rows = pooled_rows(ids_ref[start + t], len_ref[pl.ds(start + t, 1)], table_ref[slot, t])
            rows_ref[:, start + t] = rows.reshape(ndev, per, embed)

        @pl.when(step == 0)
        def _():
            pl.semaphore_wait(pltpu.get_barrier_semaphore(), ndev - 1 + nrep - 1)

        for _, peer in peers:
            remote(
                rows_ref.at[peer, pl.ds(start, CHUNK)],
                pooled_ref.at[pl.ds(emb * ntab + start, CHUNK)],
                a2a_s,
                a2a_r,
                (rep, peer),
            ).start()
        return 0

    lax.fori_loop(0, ntab // CHUNK, pool_step, 0)
    own_rows = pltpu.make_async_copy(
        rows_ref.at[emb], pooled_ref.at[pl.ds(emb * ntab, ntab)], own_sem.at[3]
    )
    own_rows.start()
    same = group_masks(per)
    own_cols = own_columns(per)
    sel_ref[...] = select_matrix(per, False)
    sel_t_ref[...] = select_matrix(per, True)
    for copy in small:
        copy.wait()
    order, again, place = scatter_index(pair_rows[...], slot_row[...])
    entries = order.shape[1]
    index_rows[0:1, 0:entries] = order
    index_rows[1:2, 0:entries] = again
    for n, row in enumerate(place):
        index_rows[2:3, n * entries : (n + 1) * entries] = row
    put_index = pltpu.make_async_copy(index_rows, index_ref, own_sem.at[8])
    put_index.start()
    own_rows.wait()
    others = pooled_ref.at[pl.ds(0, (ndev - 1) * ntab)]
    remote(others, others, a2a_s, a2a_r, mate).wait_recv()

    def gather(block, _):
        rows = [
            pooled_ref[slot_ref[block * BLK + i]].astype(jnp.float32) for i in range(BLK)
        ]
        fields_ref[block] = jnp.concatenate(rows, axis=0).astype(jnp.bfloat16)
        return 0

    lax.fori_loop(0, nblocks, gather, 0, unroll=4)

    sent = []

    def send(src, dst, send_sem, recv_sem, device):
        copy = remote(src, dst, send_sem, recv_sem, device)
        copy.start()
        sent.append(copy)

    scale = 1.0 / math.sqrt(embed)
    group = GROUP * BLK * BLK
    own = [gath.at[half, y, x, c] for half in range(nhalf)]
    for half in range(nhalf):
        for q in range(width // group):
            first = half * (NPAIR // nhalf) + q * GROUP
            left = jnp.concatenate(
                [fields_ref[pair_ref[0, first + p]] for p in range(GROUP)], axis=0
            )
            right = jnp.concatenate(
                [fields_ref[pair_ref[1, first + p]] for p in range(GROUP)], axis=0
            )
            gram = lax.dot_general(
                left, right, (((1,), (1,)), ((), ())), preferred_element_type=jnp.float32
            )
            gram = jnp.where(same, gram * scale, 0.0).astype(jnp.bfloat16)
            spread = jnp.dot(gram, sel_ref[...], preferred_element_type=jnp.float32)
            kept = jnp.where(own_cols, spread, 0.0).reshape(GROUP * BLK, per, group)
            gath[half, y, x, c, :, q * group : (q + 1) * group] = jnp.sum(kept, axis=0).astype(
                jnp.bfloat16
            )
        for k in range(1, nx):
            device = at(y, xs[k], c) if half == 0 else at(ys[k], x, c)
            send(own[half], own[half], ag1_s.at[half, k], ag1_r.at[half, k], device)
    lines = [gath.at[0, y, :, c], gath.at[1, :, x, c]]
    for half in range(nhalf):
        for k in range(1, nx):
            remote(own[half], own[half], ag1_s.at[half, k], ag1_r.at[half, k], mate).wait_recv()
        for k in range(1, nx):
            device = at(ys[k], x, c) if half == 0 else at(y, xs[k], c)
            send(lines[half], lines[half], ag2_s.at[half, k], ag2_r.at[half, k], device)
        send(lines[half], lines[half], ag3_s.at[half, 0], ag3_r.at[half, 0], mate)
    for k in range(1, nx):
        for half in range(nhalf):
            remote(lines[half], lines[half], ag2_s.at[half, k], ag2_r.at[half, k], mate).wait_recv()
            line = gath.at[0, ys[ny - k], :, c] if half == 0 else gath.at[1, :, xs[nx - k], c]
            send(line, line, ag3_s.at[half, k], ag3_r.at[half, k], mate)
    for k in range(nx):
        for half in range(nhalf):
            remote(lines[half], lines[half], ag3_s.at[half, k], ag3_r.at[half, k], mate).wait_recv()

    get_w.wait()
    get_cot.wait()
    steps = width // STEP
    pre = jnp.zeros((samples, hidden), jnp.float32)
    for half in range(nhalf):

        def forward(j, total):
            cols = pl.ds(pl.multiple_of(j * STEP, STEP), STEP)
            rows = pl.ds(pl.multiple_of(half * width + j * STEP, STEP), STEP)
            block = gath[half, :, :, :, :, cols].reshape(samples, STEP)
            return total + jnp.dot(block, w_ref[rows], preferred_element_type=jnp.float32)

        pre = lax.fori_loop(0, steps, forward, pre)
    pre = pre + b_ref[...].astype(jnp.float32)
    sig = jax.nn.sigmoid(pre)
    over_ref[...] = (pre * sig).astype(jnp.bfloat16)
    dpre = (cot_ref[...].astype(jnp.float32) * sig * (1.0 + pre * (1.0 - sig))).astype(jnp.bfloat16)

    for half in range(nhalf):

        def backward(j, _):
            cols = pl.ds(pl.multiple_of(j * STEP, STEP), STEP)
            rows = pl.ds(pl.multiple_of(half * width + j * STEP, STEP), STEP)
            block = lax.dot_general(
                dpre, w_ref[rows], (((1,), (1,)), ((), ())), preferred_element_type=jnp.float32
            )
            block = block.reshape(ny, nx, ncore, per, STEP)
            for core in range(ncore):
                part[half, core, :, :, :, cols] = block[:, :, core].astype(jnp.bfloat16)
            return 0

        lax.fori_loop(0, steps, backward, 0)
        send(part.at[half, 1 - c], xrecv.at[half], rs1_s.at[half], rs1_r.at[half], mate)

    gb = jnp.sum(dpre.astype(jnp.float32), axis=0, keepdims=True)
    bias[rep] = jnp.broadcast_to(gb, bias.shape[1:])
    for k in range(1, nrep):
        send(bias.at[rep], bias.at[rep], zb_s.at[k], zb_r.at[k], (zs[k], emb))
    quarter = gsend.shape[1]
    for half in range(nhalf):

        def weights(j, _):
            cols = pl.ds(pl.multiple_of(j * STEP, STEP), STEP)
            block = gath[half, :, :, :, :, cols].reshape(samples, STEP)
            product = lax.dot_general(
                block, dpre, (((0,), (0,)), ((), ())), preferred_element_type=jnp.float32
            )
            place = half * (width // STEP) + j
            per_quarter = quarter // STEP
            rows = pl.ds(pl.multiple_of(lax.rem(place, per_quarter) * STEP, STEP), STEP)
            gsend[place // per_quarter, rows] = product.astype(jnp.bfloat16)
            return 0

        lax.fori_loop(0, steps, weights, 0)
    for k in range(1, nrep):
        send(gsend.at[zs[k]], grecv.at[k - 1], z_s.at[k], z_r.at[k], (zs[k], emb))

    for half in range(nhalf):
        remote(xrecv.at[half], xrecv.at[half], rs1_s.at[half], rs1_r.at[half], mate).wait_recv()

        def add(j, _):
            sa[half, j] = (
                part[half, c, j].astype(jnp.float32) + xrecv[half, j].astype(jnp.float32)
            ).astype(jnp.bfloat16)
            return 0

        lax.fori_loop(0, ny, add, 0)
        for k in range(1, nx):
            if half == 0:
                src, device = sa.at[0, ys[k]], at(ys[k], x, c)
            else:
                src, device = sa.at[1, :, xs[k]], at(y, xs[k], c)
            send(src, brecv.at[half, k - 1], rs2_s.at[half, k], rs2_r.at[half, k], device)
    for half in range(nhalf):
        mine = sa[0, y] if half == 0 else sa[1, :, x]
        total = mine.astype(jnp.float32)
        for k in range(1, nx):
            slot = brecv.at[half, k - 1]
            remote(slot, slot, rs2_s.at[half, k], rs2_r.at[half, k], mate).wait_recv()
            total = total + brecv[half, k - 1].astype(jnp.float32)
        sb[half] = total.astype(jnp.bfloat16)
        for k in range(1, nx):
            place = xs[k] if half == 0 else ys[k]
            device = at(y, xs[k], c) if half == 0 else at(ys[k], x, c)
            send(
                sb.at[half, place],
                crecv.at[half, k - 1],
                rs3_s.at[half, k],
                rs3_r.at[half, k],
                device,
            )
    for half in range(nhalf):
        total = sb[half, x if half == 0 else y].astype(jnp.float32)
        for k in range(1, nx):
            slot = crecv.at[half, k - 1]
            remote(slot, slot, rs3_s.at[half, k], rs3_r.at[half, k], mate).wait_recv()
            total = total + crecv[half, k - 1].astype(jnp.float32)
        dinter_ref[:, half * width : (half + 1) * width] = total.astype(jnp.bfloat16)

    put_index.wait()
    for q in range(NPAIR // GROUP):
        left = jnp.concatenate(
            [fields_ref[pair_ref[0, q * GROUP + p]] for p in range(GROUP)], axis=0
        )
        right = jnp.concatenate(
            [fields_ref[pair_ref[1, q * GROUP + p]] for p in range(GROUP)], axis=0
        )
        entry = dinter_ref[:, q * group : (q + 1) * group].astype(jnp.float32)
        spread = jnp.broadcast_to(entry[None], (GROUP * BLK, per, group))
        spread = jnp.where(own_cols, spread.reshape(GROUP * BLK * per, group), 0.0)
        pair = jnp.dot(
            spread.astype(jnp.bfloat16), sel_t_ref[...], preferred_element_type=jnp.float32
        )
        pair = jnp.where(same, pair, 0.0).astype(jnp.bfloat16)
        to_left = jnp.dot(pair, right, preferred_element_type=jnp.float32) * scale
        to_right = (
            lax.dot_general(
                pair, left, (((0,), (0,)), ((), ())), preferred_element_type=jnp.float32
            )
            * scale
        )
        size = (GROUP, BLK * per, embed)
        contrib[q * GROUP : (q + 1) * GROUP] = to_left.reshape(size)
        contrib[NPAIR + q * GROUP : NPAIR + (q + 1) * GROUP] = to_right.reshape(size)

    def run(r, total):
        total = contrib[index_ref[0, r]] + jnp.where(index_ref[1, r] > 0, total, 0.0)
        total_ref[pl.ds(r * BLK, BLK)] = total.reshape(BLK, per, embed)
        return total

    lax.fori_loop(0, 2 * NPAIR, run, jnp.zeros((BLK * per, embed), jnp.float32), unroll=4)

    def fill(device):
        def one(t, _):
            back_ref[device, t] = total_ref[index_ref[2, device * ntab + t]].astype(jnp.bfloat16)
            return 0

        lax.fori_loop(0, ntab, one, 0, unroll=5)

    for _, peer in peers:
        fill(peer)
        remote(back_ref.at[peer], out_ref.at[emb], back_s, back_r, (rep, peer)).start()
    fill(emb)
    own_back = pltpu.make_async_copy(back_ref.at[emb], out_ref.at[emb], own_sem.at[9])
    own_back.start()

    for k in range(1, nrep):
        slot = grecv.at[k - 1]
        remote(slot, slot, z_s.at[k], z_r.at[k], mate).wait_recv()
        remote(bias.at[rep], bias.at[rep], zb_s.at[k], zb_r.at[k], mate).wait_recv()
    total = gsend[rep].astype(jnp.float32)
    for k in range(1, nrep):
        total = total + grecv[k - 1].astype(jnp.float32)
    gw_ref[...] = total.astype(jnp.bfloat16)
    for k in range(1, nrep):
        send(gw_ref, gall_ref.at[rep], za_s.at[k], za_r.at[k], (zs[k], emb))
    own_gw = pltpu.make_async_copy(gw_ref, gall_ref.at[rep], own_sem.at[10])
    own_gw.start()
    gb_ref[...] = jnp.sum(bias[...], axis=0)[:1]

    own_back.wait()
    own_gw.wait()
    for k in range(1, nrep):
        remote(gw_ref, gall_ref.at[0], za_s.at[k], za_r.at[k], mate).wait_recv()
    others = out_ref.at[pl.ds(0, ndev - 1)]
    remote(others, others, back_s, back_r, mate).wait_recv()
    sources = rows_ref.at[pl.ds(0, ndev - 1)]
    remote(sources, sources, a2a_s, a2a_r, mate).wait_send()
    sources = back_ref.at[pl.ds(0, ndev - 1)]
    remote(sources, sources, back_s, back_r, mate).wait_send()
    for copy in sent:
        copy.wait_send()


def train_step(ids, lengths, tables, field_slot, pairs, w, b, cot, grid):
    nrep, ny, nx, ncore = grid
    ndev = ny * nx * ncore
    ntab, bag, samples = ids.shape
    rows, embed = tables.shape[1:]
    per = samples // ndev
    features, hidden = w.shape
    nblocks = ndev * ntab // BLK
    nhalf, width, quarter = 2, features // 2, features // nrep
    half_rows = (nhalf, ny, nx, per, width)
    group = GROUP * BLK * BLK
    dma = pltpu.SemaphoreType.DMA
    bf16 = jnp.bfloat16
    vmem = pl.BlockSpec(memory_space=pltpu.VMEM)
    anywhere = pl.BlockSpec(memory_space=pl.ANY)
    return pl.pallas_call(
        step_kernel,
        in_specs=[anywhere, anywhere, anywhere, vmem, anywhere, anywhere, vmem, anywhere],
        out_specs=[vmem, vmem, anywhere, anywhere],
        out_shape=[
            jax.ShapeDtypeStruct((samples, hidden), bf16),
            jax.ShapeDtypeStruct((1, hidden), jnp.float32),
            jax.ShapeDtypeStruct((ndev, ntab, per, embed), bf16),
            jax.ShapeDtypeStruct((nrep, quarter, hidden), bf16),
        ],
        scratch_shapes=[
            pltpu.SMEM((ndev * ntab,), jnp.int32),
            pltpu.SMEM(pairs.shape, jnp.int32),
            pltpu.VMEM((1, ndev * ntab), jnp.int32),
            pltpu.VMEM(pairs.shape, jnp.int32),
            pltpu.VMEM((8, 1024), jnp.int32),
            pltpu.SMEM((8, 1024), jnp.int32),
            pltpu.VMEM((nblocks, BLK * per, embed), bf16),
            pltpu.VMEM((per, features), bf16),
            pltpu.VMEM((quarter, hidden), bf16),
            pltpu.VMEM((2 * NPAIR, BLK * per, embed), jnp.float32),
            pltpu.VMEM((2 * NPAIR * BLK, per, embed), jnp.float32),
            pltpu.VMEM((ndev, ntab, per, embed), bf16),
            pltpu.VMEM((ntab, bag, samples), jnp.int32),
            pltpu.VMEM((2, CHUNK, rows, embed), bf16),
            pltpu.VMEM((ndev, ntab, per, embed), bf16),
            pltpu.VMEM((ndev * ntab, per, embed), bf16),
            pltpu.VMEM((group, group), bf16),
            pltpu.VMEM((group, group), bf16),
            pltpu.VMEM((features, hidden), bf16),
            pltpu.VMEM((samples, hidden), bf16),
            pltpu.VMEM((nhalf, ny, nx, ncore, per, width), bf16),
            pltpu.VMEM((nhalf, ncore, ny, nx, per, width), bf16),
            pltpu.VMEM(half_rows, bf16),
            pltpu.VMEM(half_rows, bf16),
            pltpu.VMEM((nhalf, nx - 1, nx, per, width), bf16),
            pltpu.VMEM((nhalf, nx, per, width), bf16),
            pltpu.VMEM((nhalf, nx - 1, per, width), bf16),
            pltpu.VMEM((nrep, quarter, hidden), bf16),
            pltpu.VMEM((nrep - 1, quarter, hidden), bf16),
            pltpu.VMEM((nrep, 8, hidden), jnp.float32),
        ]
        + [dma((nhalf, nx))] * 6
        + [dma((nhalf,))] * 2
        + [dma((nhalf, nx))] * 4
        + [dma((nrep,))] * 4
        + [dma((11,)), dma((2,)), dma, dma, dma, dma, dma((nrep,)), dma((nrep,))],
        compiler_params=pltpu.CompilerParams(
            vmem_limit_bytes=60 << 20, collective_id=0, has_side_effects=True
        ),
        name="train_step",
    )(
        field_slot,
        pairs,
        ids,
        lengths,
        tables,
        w,
        b.reshape(1, hidden),
        cot,
    )


PARTS = 4


def finish_kernel(
    rows_ref,
    gall_ref,
    over_ref,
    gb_ref,
    pooled_out,
    gw_out,
    over_out,
    gb_out,
    held,
    half,
    full,
    small,
    tiny,
    sems,
):
    nrep, quarter = gall_ref.shape[:2]
    ndev = rows_ref.shape[0]
    size = ndev // PARTS
    first = [pltpu.make_async_copy(gall_ref.at[q], half.at[q], sems.at[0, q]) for q in range(nrep)]
    rows = [
        pltpu.make_async_copy(
            rows_ref.at[pl.ds(g * size, size)], held.at[pl.ds(g * size, size)], sems.at[1, g]
        )
        for g in range(PARTS)
    ]
    extra = [
        pltpu.make_async_copy(over_ref, small, sems.at[4, 0]),
        pltpu.make_async_copy(gb_ref, tiny, sems.at[4, 1]),
    ]
    for copy in [copy for two in zip(rows, first) for copy in two] + extra:
        copy.start()
    out = []
    for g in range(PARTS):
        rows[g].wait()
        for d in range(g * size, (g + 1) * size):
            pltpu.make_async_copy(held.at[d], pooled_out.at[:, d], sems.at[2, 0]).start()
        first[g].wait()
        full[g] = half[g].astype(jnp.float32)
        copy = pltpu.make_async_copy(
            full.at[g], gw_out.at[pl.ds(g * quarter, quarter)], sems.at[3, g]
        )
        copy.start()
        out.append(copy)
    for copy in extra:
        copy.wait()
    last = [
        pltpu.make_async_copy(small, over_out, sems.at[4, 2]),
        pltpu.make_async_copy(tiny, gb_out, sems.at[4, 3]),
    ]
    for copy in last:
        copy.start()
    for copy in last + out:
        copy.wait()
    pltpu.make_async_copy(pooled_out, pooled_out, sems.at[2, 0]).wait()


def finish(rows, gw_all, over, gb):
    ndev, ntab, per, embed = rows.shape
    nrep, quarter, hidden = gw_all.shape
    anywhere = pl.BlockSpec(memory_space=pl.ANY)
    return pl.pallas_call(
        finish_kernel,
        in_specs=[anywhere] * 4,
        out_specs=[anywhere] * 4,
        out_shape=[
            jax.ShapeDtypeStruct((ntab, ndev, per, embed), rows.dtype),
            jax.ShapeDtypeStruct((nrep * quarter, hidden), jnp.float32),
            jax.ShapeDtypeStruct(over.shape, over.dtype),
            jax.ShapeDtypeStruct(gb.shape, gb.dtype),
        ],
        scratch_shapes=[
            pltpu.VMEM(rows.shape, rows.dtype),
            pltpu.VMEM(gw_all.shape, gw_all.dtype),
            pltpu.VMEM(gw_all.shape, jnp.float32),
            pltpu.VMEM(over.shape, over.dtype),
            pltpu.VMEM(gb.shape, gb.dtype),
            pltpu.SemaphoreType.DMA((5, nrep)),
        ],
        compiler_params=pltpu.CompilerParams(vmem_limit_bytes=60 << 20),
        name="finish",
    )(rows, gw_all, over, gb)


def on_device(tables, bag_ids, bag_lengths, field_slot, pair_blocks, w_over, b_over, cotangent):
    grid = (lax.axis_size("rep"), 4, 4, 2)
    ids, pairs = jnp.swapaxes(bag_ids, 1, 2), pair_blocks.T
    over, gb, rows, gw_all = train_step(
        ids, bag_lengths, tables, field_slot, pairs, w_over, b_over, cotangent, grid
    )
    pooled_grad, grad_w, over_out, grad_b = finish(rows, gw_all, over, gb)
    return (
        over_out,
        grad_w,
        grad_b.reshape(b_over.shape),
        pooled_grad.reshape(tables.shape[0], bag_ids.shape[1], tables.shape[2]),
    )


def solution(mesh):
    in_specs = (
        P("emb", None, None),
        P("emb", "rep", None),
        P("emb", "rep"),
        P(),
        P(),
        P(None, "emb"),
        P("emb"),
        P("rep", "emb"),
    )
    out_specs = (P("rep", "emb"), P(None, "emb"), P("emb"), P("emb", "rep", None))
    return jax.shard_map(
        on_device, mesh=mesh, in_specs=in_specs, out_specs=out_specs, check_vma=False
    )
```

```python
import functools
import math

import jax
import jax.numpy as jnp
from jax import lax
from jax.experimental import pallas as pl
from jax.experimental.pallas import tpu as pltpu
from jax.sharding import PartitionSpec as P

BLK = 8
NPAIR = 64
GROUP = 4
WORDS = 176
BITS = 5


MESH = pl.DeviceIdType.MESH
CHUNK = 5
FIRST = 2


def remote(src, dst, send_sem, recv_sem, device):
    return pltpu.make_async_remote_copy(
        src_ref=src,
        dst_ref=dst,
        send_sem=send_sem,
        recv_sem=recv_sem,
        device_id=device,
        device_id_type=MESH,
    )


def greet(devices):
    barrier = pltpu.get_barrier_semaphore()
    for device in devices:
        pl.semaphore_signal(barrier, inc=1, device_id=device, device_id_type=MESH)


def peer_order(ny, nx, ncore):
    left = [
        (dy, dx, dc)
        for dy in range(ny)
        for dx in range(nx)
        for dc in range(ncore)
        if (dy, dx, dc) != (0, 0, 0)
    ]

    def links(offset):
        used = []
        for axis, (step, size) in enumerate(((offset[0], ny), (offset[1], nx))):
            if 0 < step <= size // 2:
                used.append(2 * axis)
            if step >= size - size // 2 and step > 0:
                used.append(2 * axis + 1)
        return used

    order, load = [], [0] * 4

    def cost(offset):
        after = list(load)
        for link in links(offset):
            after[link] += 1
        return max(after) - min(after)

    while left:
        best = min(left, key=cost)
        left.remove(best)
        order.append(best)
        for link in links(best):
            load[link] += 1
    return order


def pooled_rows(ids, lengths, table):
    bag, samples = ids.shape
    rows, embed = table.shape
    used = lax.broadcasted_iota(jnp.int32, (bag, samples), 0) < lengths
    field = ids // WORDS
    word = ids - field * WORDS
    value = jnp.where(used, jnp.left_shift(1, field * BITS), 0)
    halves = []
    for half in range(samples // 128):
        lanes = slice(half * 128, half * 128 + 128)
        row = lax.broadcasted_iota(jnp.int32, (WORDS, 128), 0)
        total = jnp.zeros((WORDS, 128), jnp.int32)
        for k in range(bag):
            total += jnp.where(row == word[k : k + 1, lanes], value[k : k + 1, lanes], 0)
        halves.append(total)
    counts = jnp.concatenate(halves, axis=1)
    chunks = []
    for part, start in enumerate(range(0, rows, WORDS)):
        chunk = (counts[: min(WORDS, rows - start)] >> (BITS * part)) & ((1 << BITS) - 1)
        chunks.append(chunk.astype(jnp.float32).astype(jnp.bfloat16))
    pooled = lax.dot_general(
        table,
        jnp.concatenate(chunks, axis=0),
        (((0,), (0,)), ((), ())),
        preferred_element_type=jnp.float32,
    )
    return pooled.T.astype(jnp.bfloat16)


def group_masks(samples):
    n = GROUP * BLK * samples
    r = lax.broadcasted_iota(jnp.int32, (n, n), 0)
    c = lax.broadcasted_iota(jnp.int32, (n, n), 1)
    per = BLK * samples
    same = (r // per == c // per) & (r % samples == c % samples)
    return same


def select_matrix(samples, transposed):
    rows, cols = GROUP * BLK * samples, GROUP * BLK * BLK
    shape = (cols, rows) if transposed else (rows, cols)
    r = lax.broadcasted_iota(jnp.int32, shape, 1 if transposed else 0)
    c = lax.broadcasted_iota(jnp.int32, shape, 0 if transposed else 1)
    hit = (r // (BLK * samples) == c // (BLK * BLK)) & ((r // samples) % BLK == c % BLK)
    return jnp.where(hit, 1.0, 0.0).astype(jnp.bfloat16)


def own_columns(samples):
    rows, cols = GROUP * BLK * samples, GROUP * BLK * BLK
    r = lax.broadcasted_iota(jnp.int32, (rows, cols), 0)
    c = lax.broadcasted_iota(jnp.int32, (rows, cols), 1)
    return r // samples == c // BLK


STEP = 512


def scatter_index(pair_rows, slots):
    entries, nfields = 2 * pair_rows.shape[1], slots.shape[1]
    block = jnp.concatenate([pair_rows[0:1], pair_rows[1:2]], axis=1)
    square = (entries, entries)
    down = lax.broadcasted_iota(jnp.int32, square, 0)
    across = lax.broadcasted_iota(jnp.int32, square, 1)
    of_col = jnp.broadcast_to(block, square)
    of_row = of_col.T
    earlier = (of_row == of_col) & (down < across)
    rank = jnp.sum(jnp.where((of_row < of_col) | earlier, 1, 0), axis=0, keepdims=True)
    repeat = jnp.sum(jnp.where(earlier, 1, 0), axis=0, keepdims=True)
    hit = jnp.broadcast_to(rank, square).T == across
    order = jnp.sum(jnp.where(hit, down, 0), axis=0, keepdims=True)
    again = jnp.sum(jnp.where(hit, jnp.broadcast_to(repeat, square).T, 0), axis=0, keepdims=True)

    wide = (entries, nfields)
    own_block = lax.broadcasted_iota(jnp.int32, wide, 1) // BLK
    upto = jnp.where(of_row[:, :1] <= own_block, 1, 0)
    last = jnp.sum(upto, axis=0, keepdims=True) - 1
    piece = last * BLK + lax.broadcasted_iota(jnp.int32, (1, nfields), 1) % BLK
    places = []
    for start in range(0, nfields, entries):
        slot = lax.broadcasted_iota(jnp.int32, wide, 0) + start
        found = jnp.sum(jnp.where(slot == slots, piece, 0), axis=1, keepdims=True)
        row = jnp.broadcast_to(found, square).T
        places.append(jnp.clip(row[0:1], 0, entries * BLK - 1))
    return jnp.clip(order, 0, entries - 1), again, places


def step_kernel(
    slot_hbm,
    pair_hbm,
    ids_hbm,
    len_ref,
    tables_hbm,
    w_hbm,
    b_ref,
    cot_hbm,
    over_ref,
    gb_ref,
    out_ref,
    gall_ref,
    slot_ref,
    pair_ref,
    slot_row,
    pair_rows,
    index_rows,
    index_ref,
    fields_ref,
    dinter_ref,
    gw_ref,
    contrib,
    total_ref,
    back_ref,
    ids_ref,
    table_ref,
    rows_ref,
    pooled_ref,
    sel_ref,
    sel_t_ref,
    w_ref,
    cot_ref,
    gath,
    part,
    xrecv,
    sa,
    brecv,
    sb,
    crecv,
    gsend,
    grecv,
    bias,
    ag1_s,
    ag1_r,
    ag2_s,
    ag2_r,
    ag3_s,
    ag3_r,
    rs1_s,
    rs1_r,
    rs2_s,
    rs2_r,
    rs3_s,
    rs3_r,
    z_s,
    z_r,
    zb_s,
    zb_r,
    own_sem,
    table_sem,
    a2a_s,
    a2a_r,
    back_s,
    back_r,
    za_s,
    za_r,
):
    nhalf, ny, nx, ncore, per, width = gath.shape
    nrep = gsend.shape[0]
    samples = ny * nx * ncore * per
    hidden = w_ref.shape[1]
    rep, emb = lax.axis_index("rep"), lax.axis_index("emb")
    y, x, c = emb // (nx * ncore), lax.rem(emb // ncore, nx), lax.rem(emb, ncore)

    def at(yy, xx, cc):
        return (rep, (yy * nx + xx) * ncore + cc)

    xs = [lax.rem(x + k, nx) for k in range(nx)]
    ys = [lax.rem(y + k, ny) for k in range(ny)]
    zs = [lax.rem(rep + k, nrep) for k in range(nrep)]
    mate = at(y, x, 1 - c)
    peers = [
        at(ys[dy], xs[dx], lax.rem(c + dc, ncore)) for dy, dx, dc in peer_order(ny, nx, ncore)
    ]
    ndev, ntab, _, embed = rows_ref.shape
    nblocks = fields_ref.shape[0]

    get_ids = pltpu.make_async_copy(ids_hbm, ids_ref, own_sem.at[0])
    get_ids.start()
    small = [
        pltpu.make_async_copy(slot_hbm, slot_ref, own_sem.at[4]),
        pltpu.make_async_copy(pair_hbm, pair_ref, own_sem.at[5]),
        pltpu.make_async_copy(slot_hbm, slot_row.at[0], own_sem.at[6]),
        pltpu.make_async_copy(pair_hbm, pair_rows, own_sem.at[7]),
    ]
    for copy in small:
        copy.start()

    def get_tables(start, size, slot):
        return pltpu.make_async_copy(
            tables_hbm.at[pl.ds(start, size)],
            table_ref.at[slot, pl.ds(0, size)],
            table_sem.at[slot],
        )

    middle = (ntab - FIRST) // CHUNK
    rest = ntab - FIRST - middle * CHUNK
    get_tables(0, FIRST, 0).start()
    get_tables(FIRST, CHUNK, 1).start()
    get_w = pltpu.make_async_copy(w_hbm, w_ref, own_sem.at[1])
    get_w.start()
    get_cot = pltpu.make_async_copy(cot_hbm, cot_ref, own_sem.at[2])
    get_cot.start()
    greet(peers)
    greet([(zs[k], emb) for k in range(1, nrep)])
    get_ids.wait()

    def pool_tables(start, size, slot):
        for t in range(size):
            rows = pooled_rows(ids_ref[start + t], len_ref[pl.ds(start + t, 1)], table_ref[slot, t])
            rows_ref[:, start + t] = rows.reshape(ndev, per, embed)

    def send_rows(start, size):
        for _, peer in peers:
            remote(
                rows_ref.at[peer, pl.ds(start, size)],
                pooled_ref.at[pl.ds(emb * ntab + start, size)],
                a2a_s,
                a2a_r,
                (rep, peer),
            ).start()

    def pool_step(step, _):
        start = FIRST + step * CHUNK
        slot = lax.rem(step + 1, 2)
        get_tables(start, CHUNK, slot).wait()

        @pl.when(step + 1 < middle)
        def _():
            get_tables(start + CHUNK, CHUNK, 1 - slot).start()

        @pl.when(step + 1 == middle)
        def _():
            get_tables(ntab - rest, rest, 1 - slot).start()

        pool_tables(start, CHUNK, slot)
        send_rows(start, CHUNK)
        return 0

    get_tables(0, FIRST, 0).wait()
    pool_tables(0, FIRST, 0)
    pl.semaphore_wait(pltpu.get_barrier_semaphore(), ndev - 1 + nrep - 1)
    send_rows(0, FIRST)
    lax.fori_loop(0, middle, pool_step, 0)
    last_slot = (middle + 1) % 2
    get_tables(ntab - rest, rest, last_slot).wait()
    pool_tables(ntab - rest, rest, last_slot)
    send_rows(ntab - rest, rest)
    own_rows = pltpu.make_async_copy(
        rows_ref.at[emb], pooled_ref.at[pl.ds(emb * ntab, ntab)], own_sem.at[3]
    )
    own_rows.start()
    same = group_masks(per)
    own_cols = own_columns(per)
    sel_ref[...] = select_matrix(per, False)
    sel_t_ref[...] = select_matrix(per, True)
    for copy in small:
        copy.wait()
    order, again, place = scatter_index(pair_rows[...], slot_row[...])
    entries = order.shape[1]
    index_rows[0:1, 0:entries] = order
    index_rows[1:2, 0:entries] = again
    for n, row in enumerate(place):
        index_rows[2:3, n * entries : (n + 1) * entries] = row
    put_index = pltpu.make_async_copy(index_rows, index_ref, own_sem.at[8])
    put_index.start()
    own_rows.wait()
    others = pooled_ref.at[pl.ds(0, (ndev - 1) * ntab)]
    remote(others, others, a2a_s, a2a_r, mate).wait_recv()

    def gather(block, _):
        rows = [
            pooled_ref[slot_ref[block * BLK + i]].astype(jnp.float32) for i in range(BLK)
        ]
        fields_ref[block] = jnp.concatenate(rows, axis=0).astype(jnp.bfloat16)
        return 0

    lax.fori_loop(0, nblocks, gather, 0, unroll=4)

    sent = []

    def send(src, dst, send_sem, recv_sem, device, keep=True):
        copy = remote(src, dst, send_sem, recv_sem, device)
        copy.start()
        if keep:
            sent.append(copy)

    scale = 1.0 / math.sqrt(embed)
    group = GROUP * BLK * BLK
    own = [gath.at[half, y, x, c] for half in range(nhalf)]
    for half in range(nhalf):
        for q in range(width // group):
            first = half * (NPAIR // nhalf) + q * GROUP
            left = jnp.concatenate(
                [fields_ref[pair_ref[0, first + p]] for p in range(GROUP)], axis=0
            )
            right = jnp.concatenate(
                [fields_ref[pair_ref[1, first + p]] for p in range(GROUP)], axis=0
            )
            gram = lax.dot_general(
                left, right, (((1,), (1,)), ((), ())), preferred_element_type=jnp.float32
            )
            gram = jnp.where(same, gram * scale, 0.0).astype(jnp.bfloat16)
            spread = jnp.dot(gram, sel_ref[...], preferred_element_type=jnp.float32)
            kept = jnp.where(own_cols, spread, 0.0).reshape(GROUP * BLK, per, group)
            gath[half, y, x, c, :, q * group : (q + 1) * group] = jnp.sum(kept, axis=0).astype(
                jnp.bfloat16
            )
        for k in range(1, nx):
            near = at(y, xs[k], c) if half == 0 else at(ys[k], x, c)
            far = at(ys[k], x, c) if half == 0 else at(y, xs[k], c)
            send(own[half], own[half], ag1_s.at[half, k], ag1_r.at[half, k], near)
            send(own[half], own[half], ag2_s.at[half, k], ag2_r.at[half, k], far, False)
        send(own[half], own[half], ag3_s.at[half, 0], ag3_r.at[half, 0], mate, False)
    lines = [gath.at[0, y, :, c], gath.at[1, :, x, c]]
    for k in [1, nx - 1] + list(range(2, nx - 1)):
        for half in range(nhalf):
            block = gath.at[0, y, xs[nx - k], c] if half == 0 else gath.at[1, ys[ny - k], x, c]
            remote(block, block, ag1_s.at[half, k], ag1_r.at[half, k], mate).wait_recv()
            for j in range(1, nx):
                far = at(ys[j], x, c) if half == 0 else at(y, xs[j], c)
                send(block, block, ag2_s.at[half, j], ag2_r.at[half, j], far, False)
            send(block, block, ag3_s.at[half, 0], ag3_r.at[half, 0], mate, False)
    for k in [1, nx - 1] + list(range(2, nx - 1)):
        for half in range(nhalf):
            remote(lines[half], lines[half], ag2_s.at[half, k], ag2_r.at[half, k], mate).wait_recv()
            line = gath.at[0, ys[ny - k], :, c] if half == 0 else gath.at[1, :, xs[nx - k], c]
            send(line, line, ag3_s.at[half, k], ag3_r.at[half, k], mate)
    get_w.wait()
    get_cot.wait()
    steps = width // STEP
    pre = jnp.zeros((samples, hidden), jnp.float32)
    for half in range(nhalf):
        for k in range(nx):
            remote(lines[half], lines[half], ag3_s.at[half, k], ag3_r.at[half, k], mate).wait_recv()

        def forward(j, total):
            cols = pl.ds(pl.multiple_of(j * STEP, STEP), STEP)
            rows = pl.ds(pl.multiple_of(half * width + j * STEP, STEP), STEP)
            block = gath[half, :, :, :, :, cols].reshape(samples, STEP)
            return total + jnp.dot(block, w_ref[rows], preferred_element_type=jnp.float32)

        pre = lax.fori_loop(0, steps, forward, pre)
    pre = pre + b_ref[...].astype(jnp.float32)
    sig = jax.nn.sigmoid(pre)
    over_ref[...] = (pre * sig).astype(jnp.bfloat16)
    dpre = (cot_ref[...].astype(jnp.float32) * sig * (1.0 + pre * (1.0 - sig))).astype(jnp.bfloat16)

    for half in range(nhalf):

        def backward(j, _):
            cols = pl.ds(pl.multiple_of(j * STEP, STEP), STEP)
            rows = pl.ds(pl.multiple_of(half * width + j * STEP, STEP), STEP)
            block = lax.dot_general(
                dpre, w_ref[rows], (((1,), (1,)), ((), ())), preferred_element_type=jnp.float32
            )
            block = block.reshape(ny, nx, ncore, per, STEP)
            for core in range(ncore):
                part[half, core, :, :, :, cols] = block[:, :, core].astype(jnp.bfloat16)
            return 0

        lax.fori_loop(0, steps, backward, 0)
        send(part.at[half, 1 - c], xrecv.at[half], rs1_s.at[half], rs1_r.at[half], mate)

    for half in range(nhalf):
        remote(xrecv.at[half], xrecv.at[half], rs1_s.at[half], rs1_r.at[half], mate).wait_recv()

        def add(j, _):
            sa[half, j] = (
                part[half, c, j].astype(jnp.float32) + xrecv[half, j].astype(jnp.float32)
            ).astype(jnp.bfloat16)
            return 0

        lax.fori_loop(0, ny, add, 0)
        for k in range(1, nx):
            if half == 0:
                src, device = sa.at[0, ys[k]], at(ys[k], x, c)
            else:
                src, device = sa.at[1, :, xs[k]], at(y, xs[k], c)
            send(src, brecv.at[half, k - 1], rs2_s.at[half, k], rs2_r.at[half, k], device)
    gb = jnp.sum(dpre.astype(jnp.float32), axis=0, keepdims=True)
    bias[rep] = jnp.broadcast_to(gb, bias.shape[1:])
    for k in range(1, nrep):
        send(bias.at[rep], bias.at[rep], zb_s.at[k], zb_r.at[k], (zs[k], emb))
    quarter = gsend.shape[1]
    for half in range(nhalf):

        def weights(j, _):
            cols = pl.ds(pl.multiple_of(j * STEP, STEP), STEP)
            block = gath[half, :, :, :, :, cols].reshape(samples, STEP)
            product = lax.dot_general(
                block, dpre, (((0,), (0,)), ((), ())), preferred_element_type=jnp.float32
            )
            place = half * (width // STEP) + j
            per_quarter = quarter // STEP
            rows = pl.ds(pl.multiple_of(lax.rem(place, per_quarter) * STEP, STEP), STEP)
            gsend[place // per_quarter, rows] = product.astype(jnp.bfloat16)
            return 0

        lax.fori_loop(0, steps, weights, 0)
    for k in range(1, nrep):
        send(gsend.at[zs[k]], grecv.at[k - 1], z_s.at[k], z_r.at[k], (zs[k], emb))

    for half in range(nhalf):
        mine = sa[0, y] if half == 0 else sa[1, :, x]
        total = mine.astype(jnp.float32)
        for k in range(1, nx):
            slot = brecv.at[half, k - 1]
            remote(slot, slot, rs2_s.at[half, k], rs2_r.at[half, k], mate).wait_recv()
            total = total + brecv[half, k - 1].astype(jnp.float32)
        sb[half] = total.astype(jnp.bfloat16)
        for k in range(1, nx):
            place = xs[k] if half == 0 else ys[k]
            device = at(y, xs[k], c) if half == 0 else at(ys[k], x, c)
            send(
                sb.at[half, place],
                crecv.at[half, k - 1],
                rs3_s.at[half, k],
                rs3_r.at[half, k],
                device,
            )
    for half in range(nhalf):
        total = sb[half, x if half == 0 else y].astype(jnp.float32)
        for k in range(1, nx):
            slot = crecv.at[half, k - 1]
            remote(slot, slot, rs3_s.at[half, k], rs3_r.at[half, k], mate).wait_recv()
            total = total + crecv[half, k - 1].astype(jnp.float32)
        dinter_ref[:, half * width : (half + 1) * width] = total.astype(jnp.bfloat16)

    put_index.wait()
    for q in range(NPAIR // GROUP):
        left = jnp.concatenate(
            [fields_ref[pair_ref[0, q * GROUP + p]] for p in range(GROUP)], axis=0
        )
        right = jnp.concatenate(
            [fields_ref[pair_ref[1, q * GROUP + p]] for p in range(GROUP)], axis=0
        )
        entry = dinter_ref[:, q * group : (q + 1) * group].astype(jnp.float32)
        spread = jnp.broadcast_to(entry[None], (GROUP * BLK, per, group))
        spread = jnp.where(own_cols, spread.reshape(GROUP * BLK * per, group), 0.0)
        pair = jnp.dot(
            spread.astype(jnp.bfloat16), sel_t_ref[...], preferred_element_type=jnp.float32
        )
        pair = jnp.where(same, pair, 0.0).astype(jnp.bfloat16)
        to_left = jnp.dot(pair, right, preferred_element_type=jnp.float32) * scale
        to_right = (
            lax.dot_general(
                pair, left, (((0,), (0,)), ((), ())), preferred_element_type=jnp.float32
            )
            * scale
        )
        size = (GROUP, BLK * per, embed)
        contrib[q * GROUP : (q + 1) * GROUP] = to_left.reshape(size)
        contrib[NPAIR + q * GROUP : NPAIR + (q + 1) * GROUP] = to_right.reshape(size)

    def run(r, total):
        total = contrib[index_ref[0, r]] + jnp.where(index_ref[1, r] > 0, total, 0.0)
        total_ref[pl.ds(r * BLK, BLK)] = total.reshape(BLK, per, embed)
        return total

    lax.fori_loop(0, 2 * NPAIR, run, jnp.zeros((BLK * per, embed), jnp.float32), unroll=4)

    def fill(device):
        def one(t, _):
            back_ref[device, t] = total_ref[index_ref[2, device * ntab + t]].astype(jnp.bfloat16)
            return 0

        lax.fori_loop(0, ntab, one, 0, unroll=5)

    for _, peer in peers:
        fill(peer)
        remote(back_ref.at[peer], out_ref.at[emb], back_s, back_r, (rep, peer)).start()
    fill(emb)
    own_back = pltpu.make_async_copy(back_ref.at[emb], out_ref.at[emb], own_sem.at[9])
    own_back.start()

    for k in range(1, nrep):
        slot = grecv.at[k - 1]
        remote(slot, slot, z_s.at[k], z_r.at[k], mate).wait_recv()
        remote(bias.at[rep], bias.at[rep], zb_s.at[k], zb_r.at[k], mate).wait_recv()
    total = gsend[rep].astype(jnp.float32)
    for k in range(1, nrep):
        total = total + grecv[k - 1].astype(jnp.float32)
    gw_ref[...] = total.astype(jnp.bfloat16)
    for k in range(1, nrep):
        send(gw_ref, gall_ref.at[rep], za_s.at[k], za_r.at[k], (zs[k], emb))
    own_gw = pltpu.make_async_copy(gw_ref, gall_ref.at[rep], own_sem.at[10])
    own_gw.start()
    gb_ref[...] = jnp.sum(bias[...], axis=0)[:1]

    own_back.wait()
    own_gw.wait()
    for k in range(1, nrep):
        remote(gw_ref, gall_ref.at[0], za_s.at[k], za_r.at[k], mate).wait_recv()
    others = out_ref.at[pl.ds(0, ndev - 1)]
    remote(others, others, back_s, back_r, mate).wait_recv()
    sources = rows_ref.at[pl.ds(0, ndev - 1)]
    remote(sources, sources, a2a_s, a2a_r, mate).wait_send()
    sources = back_ref.at[pl.ds(0, ndev - 1)]
    remote(sources, sources, back_s, back_r, mate).wait_send()
    for half in range(nhalf):
        line = lines[half]
        for k in range(1, nx):
            remote(line, line, ag2_s.at[half, k], ag2_r.at[half, k], mate).wait_send()
        remote(line, line, ag3_s.at[half, 0], ag3_r.at[half, 0], mate).wait_send()
    for copy in sent:
        copy.wait_send()


def train_step(ids, lengths, tables, field_slot, pairs, w, b, cot, grid):
    nrep, ny, nx, ncore = grid
    ndev = ny * nx * ncore
    ntab, bag, samples = ids.shape
    rows, embed = tables.shape[1:]
    per = samples // ndev
    features, hidden = w.shape
    nblocks = ndev * ntab // BLK
    nhalf, width, quarter = 2, features // 2, features // nrep
    half_rows = (nhalf, ny, nx, per, width)
    group = GROUP * BLK * BLK
    dma = pltpu.SemaphoreType.DMA
    bf16 = jnp.bfloat16
    vmem = pl.BlockSpec(memory_space=pltpu.VMEM)
    anywhere = pl.BlockSpec(memory_space=pl.ANY)
    return pl.pallas_call(
        step_kernel,
        in_specs=[anywhere, anywhere, anywhere, vmem, anywhere, anywhere, vmem, anywhere],
        out_specs=[vmem, vmem, anywhere, anywhere],
        out_shape=[
            jax.ShapeDtypeStruct((samples, hidden), bf16),
            jax.ShapeDtypeStruct((1, hidden), jnp.float32),
            jax.ShapeDtypeStruct((ndev, ntab, per, embed), bf16),
            jax.ShapeDtypeStruct((nrep, quarter, hidden), bf16),
        ],
        scratch_shapes=[
            pltpu.SMEM((ndev * ntab,), jnp.int32),
            pltpu.SMEM(pairs.shape, jnp.int32),
            pltpu.VMEM((1, ndev * ntab), jnp.int32),
            pltpu.VMEM(pairs.shape, jnp.int32),
            pltpu.VMEM((8, 1024), jnp.int32),
            pltpu.SMEM((8, 1024), jnp.int32),
            pltpu.VMEM((nblocks, BLK * per, embed), bf16),
            pltpu.VMEM((per, features), bf16),
            pltpu.VMEM((quarter, hidden), bf16),
            pltpu.VMEM((2 * NPAIR, BLK * per, embed), jnp.float32),
            pltpu.VMEM((2 * NPAIR * BLK, per, embed), jnp.float32),
            pltpu.VMEM((ndev, ntab, per, embed), bf16),
            pltpu.VMEM((ntab, bag, samples), jnp.int32),
            pltpu.VMEM((2, CHUNK, rows, embed), bf16),
            pltpu.VMEM((ndev, ntab, per, embed), bf16),
            pltpu.VMEM((ndev * ntab, per, embed), bf16),
            pltpu.VMEM((group, group), bf16),
            pltpu.VMEM((group, group), bf16),
            pltpu.VMEM((features, hidden), bf16),
            pltpu.VMEM((samples, hidden), bf16),
            pltpu.VMEM((nhalf, ny, nx, ncore, per, width), bf16),
            pltpu.VMEM((nhalf, ncore, ny, nx, per, width), bf16),
            pltpu.VMEM(half_rows, bf16),
            pltpu.VMEM(half_rows, bf16),
            pltpu.VMEM((nhalf, nx - 1, nx, per, width), bf16),
            pltpu.VMEM((nhalf, nx, per, width), bf16),
            pltpu.VMEM((nhalf, nx - 1, per, width), bf16),
            pltpu.VMEM((nrep, quarter, hidden), bf16),
            pltpu.VMEM((nrep - 1, quarter, hidden), bf16),
            pltpu.VMEM((nrep, 8, hidden), jnp.float32),
        ]
        + [dma((nhalf, nx))] * 6
        + [dma((nhalf,))] * 2
        + [dma((nhalf, nx))] * 4
        + [dma((nrep,))] * 4
        + [dma((11,)), dma((2,)), dma, dma, dma, dma, dma((nrep,)), dma((nrep,))],
        compiler_params=pltpu.CompilerParams(
            vmem_limit_bytes=60 << 20, collective_id=0, has_side_effects=True
        ),
        name="train_step",
    )(
        field_slot,
        pairs,
        ids,
        lengths,
        tables,
        w,
        b.reshape(1, hidden),
        cot,
    )


PARTS = 4


def finish_kernel(
    rows_ref,
    gall_ref,
    over_ref,
    gb_ref,
    pooled_out,
    gw_out,
    over_out,
    gb_out,
    held,
    half,
    full,
    small,
    tiny,
    sems,
):
    nrep, quarter = gall_ref.shape[:2]
    ndev = rows_ref.shape[0]
    size = ndev // PARTS
    first = [pltpu.make_async_copy(gall_ref.at[q], half.at[q], sems.at[0, q]) for q in range(nrep)]
    rows = [
        pltpu.make_async_copy(
            rows_ref.at[pl.ds(g * size, size)], held.at[pl.ds(g * size, size)], sems.at[1, g]
        )
        for g in range(PARTS)
    ]
    extra = [
        pltpu.make_async_copy(over_ref, small, sems.at[4, 0]),
        pltpu.make_async_copy(gb_ref, tiny, sems.at[4, 1]),
    ]
    for copy in [copy for two in zip(rows, first) for copy in two] + extra:
        copy.start()
    out = []
    for g in range(PARTS):
        rows[g].wait()
        for d in range(g * size, (g + 1) * size):
            pltpu.make_async_copy(held.at[d], pooled_out.at[:, d], sems.at[2, 0]).start()
        first[g].wait()
        full[g] = half[g].astype(jnp.float32)
        copy = pltpu.make_async_copy(
            full.at[g], gw_out.at[pl.ds(g * quarter, quarter)], sems.at[3, g]
        )
        copy.start()
        out.append(copy)
    for copy in extra:
        copy.wait()
    last = [
        pltpu.make_async_copy(small, over_out, sems.at[4, 2]),
        pltpu.make_async_copy(tiny, gb_out, sems.at[4, 3]),
    ]
    for copy in last:
        copy.start()
    for copy in last + out:
        copy.wait()
    pltpu.make_async_copy(pooled_out, pooled_out, sems.at[2, 0]).wait()


def finish(rows, gw_all, over, gb):
    ndev, ntab, per, embed = rows.shape
    nrep, quarter, hidden = gw_all.shape
    anywhere = pl.BlockSpec(memory_space=pl.ANY)
    return pl.pallas_call(
        finish_kernel,
        in_specs=[anywhere] * 4,
        out_specs=[anywhere] * 4,
        out_shape=[
            jax.ShapeDtypeStruct((ntab, ndev, per, embed), rows.dtype),
            jax.ShapeDtypeStruct((nrep * quarter, hidden), jnp.float32),
            jax.ShapeDtypeStruct(over.shape, over.dtype),
            jax.ShapeDtypeStruct(gb.shape, gb.dtype),
        ],
        scratch_shapes=[
            pltpu.VMEM(rows.shape, rows.dtype),
            pltpu.VMEM(gw_all.shape, gw_all.dtype),
            pltpu.VMEM(gw_all.shape, jnp.float32),
            pltpu.VMEM(over.shape, over.dtype),
            pltpu.VMEM(gb.shape, gb.dtype),
            pltpu.SemaphoreType.DMA((5, nrep)),
        ],
        compiler_params=pltpu.CompilerParams(vmem_limit_bytes=60 << 20),
        name="finish",
    )(rows, gw_all, over, gb)


def on_device(tables, bag_ids, bag_lengths, field_slot, pair_blocks, w_over, b_over, cotangent):
    grid = (lax.axis_size("rep"), 4, 4, 2)
    ids, pairs = jnp.swapaxes(bag_ids, 1, 2), pair_blocks.T
    over, gb, rows, gw_all = train_step(
        ids, bag_lengths, tables, field_slot, pairs, w_over, b_over, cotangent, grid
    )
    pooled_grad, grad_w, over_out, grad_b = finish(rows, gw_all, over, gb)
    return (
        over_out,
        grad_w,
        grad_b.reshape(b_over.shape),
        pooled_grad.reshape(tables.shape[0], bag_ids.shape[1], tables.shape[2]),
    )


def solution(mesh):
    in_specs = (
        P("emb", None, None),
        P("emb", "rep", None),
        P("emb", "rep"),
        P(),
        P(),
        P(None, "emb"),
        P("emb"),
        P("rep", "emb"),
    )
    out_specs = (P("rep", "emb"), P(None, "emb"), P("emb"), P("emb", "rep", None))
    return jax.shard_map(
        on_device, mesh=mesh, in_specs=in_specs, out_specs=out_specs, check_vma=False
    )
```

```python
import functools
import math

import jax
import jax.numpy as jnp
from jax import lax
from jax.experimental import pallas as pl
from jax.experimental.pallas import tpu as pltpu
from jax.sharding import PartitionSpec as P

BLK = 8
NPAIR = 64
GROUP = 4
WORDS = 128
BITS = 4
NIBBLES = 0x0F0F0F0F


MESH = pl.DeviceIdType.MESH
TABLES = (5, 8, 8, 4)


def remote(src, dst, send_sem, recv_sem, device):
    return pltpu.make_async_remote_copy(
        src_ref=src,
        dst_ref=dst,
        send_sem=send_sem,
        recv_sem=recv_sem,
        device_id=device,
        device_id_type=MESH,
    )


def greet(devices):
    barrier = pltpu.get_barrier_semaphore()
    for device in devices:
        pl.semaphore_signal(barrier, inc=1, device_id=device, device_id_type=MESH)


def peer_order(ny, nx, ncore):
    left = [
        (dy, dx, dc)
        for dy in range(ny)
        for dx in range(nx)
        for dc in range(ncore)
        if (dy, dx, dc) != (0, 0, 0)
    ]

    def links(offset):
        used = []
        for axis, (step, size) in enumerate(((offset[0], ny), (offset[1], nx))):
            if 0 < step <= size // 2:
                used.append(2 * axis)
            if step >= size - size // 2 and step > 0:
                used.append(2 * axis + 1)
        return used

    order, load = [], [0] * 4

    def cost(offset):
        after = list(load)
        for link in links(offset):
            after[link] += 1
        return max(after) - min(after)

    while left:
        best = min(left, key=cost)
        left.remove(best)
        order.append(best)
        for link in links(best):
            load[link] += 1
    return order


def pooled_rows(ids, lengths, table):
    bag, samples = ids.shape
    used = lax.broadcasted_iota(jnp.int32, (bag, samples), 0) < lengths
    word = ids & (WORDS - 1)
    value = jnp.where(used, jnp.left_shift(1, (ids // WORDS) * BITS), 0)
    lows, highs = [], []
    for half in range(samples // 128):
        lanes = slice(half * 128, half * 128 + 128)
        row = lax.broadcasted_iota(jnp.int32, (WORDS, 128), 0)
        low, high = None, None
        for first in range(0, bag, 8):
            total = None
            for k in range(first, first + 8):
                hit = jnp.where(row == word[k : k + 1, lanes], value[k : k + 1, lanes], 0)
                total = hit if total is None else total + hit
            even, odd = total & NIBBLES, (total >> BITS) & NIBBLES
            low = even if low is None else low + even
            high = odd if high is None else high + odd
        lows.append(low)
        highs.append(high)
    bytes_of = [jnp.concatenate(lows, axis=1), jnp.concatenate(highs, axis=1)]
    chunks = []
    for part in range(table.shape[0] // WORDS):
        chunk = (bytes_of[part % 2] >> (8 * (part // 2))) & 31
        chunks.append(chunk.astype(jnp.float32).astype(jnp.bfloat16))
    pooled = lax.dot_general(
        table,
        jnp.concatenate(chunks, axis=0),
        (((0,), (0,)), ((), ())),
        preferred_element_type=jnp.float32,
    )
    return pooled.T.astype(jnp.bfloat16)


def group_masks(samples):
    n = GROUP * BLK * samples
    r = lax.broadcasted_iota(jnp.int32, (n, n), 0)
    c = lax.broadcasted_iota(jnp.int32, (n, n), 1)
    per = BLK * samples
    same = (r // per == c // per) & (r % samples == c % samples)
    return same


def select_matrix(samples, transposed):
    rows, cols = GROUP * BLK * samples, GROUP * BLK * BLK
    shape = (cols, rows) if transposed else (rows, cols)
    r = lax.broadcasted_iota(jnp.int32, shape, 1 if transposed else 0)
    c = lax.broadcasted_iota(jnp.int32, shape, 0 if transposed else 1)
    hit = (r // (BLK * samples) == c // (BLK * BLK)) & ((r // samples) % BLK == c % BLK)
    return jnp.where(hit, 1.0, 0.0).astype(jnp.bfloat16)


def own_columns(samples):
    rows, cols = GROUP * BLK * samples, GROUP * BLK * BLK
    r = lax.broadcasted_iota(jnp.int32, (rows, cols), 0)
    c = lax.broadcasted_iota(jnp.int32, (rows, cols), 1)
    return r // samples == c // BLK


STEP = 512


def scatter_index(pair_rows, slots):
    entries, nfields = 2 * pair_rows.shape[1], slots.shape[1]
    block = jnp.concatenate([pair_rows[0:1], pair_rows[1:2]], axis=1)
    square = (entries, entries)
    down = lax.broadcasted_iota(jnp.int32, square, 0)
    across = lax.broadcasted_iota(jnp.int32, square, 1)
    of_col = jnp.broadcast_to(block, square)
    of_row = of_col.T
    earlier = (of_row == of_col) & (down < across)
    rank = jnp.sum(jnp.where((of_row < of_col) | earlier, 1, 0), axis=0, keepdims=True)
    repeat = jnp.sum(jnp.where(earlier, 1, 0), axis=0, keepdims=True)
    hit = jnp.broadcast_to(rank, square).T == across
    order = jnp.sum(jnp.where(hit, down, 0), axis=0, keepdims=True)
    again = jnp.sum(jnp.where(hit, jnp.broadcast_to(repeat, square).T, 0), axis=0, keepdims=True)

    wide = (entries, nfields)
    own_block = lax.broadcasted_iota(jnp.int32, wide, 1) // BLK
    upto = jnp.where(of_row[:, :1] <= own_block, 1, 0)
    last = jnp.sum(upto, axis=0, keepdims=True) - 1
    piece = last * BLK + lax.broadcasted_iota(jnp.int32, (1, nfields), 1) % BLK
    places = []
    for start in range(0, nfields, entries):
        slot = lax.broadcasted_iota(jnp.int32, wide, 0) + start
        found = jnp.sum(jnp.where(slot == slots, piece, 0), axis=1, keepdims=True)
        row = jnp.broadcast_to(found, square).T
        places.append(jnp.clip(row[0:1], 0, entries * BLK - 1))
    return jnp.clip(order, 0, entries - 1), again, places


def step_kernel(
    slot_hbm,
    pair_hbm,
    ids_hbm,
    len_ref,
    tables_hbm,
    w_hbm,
    b_ref,
    cot_hbm,
    over_ref,
    gb_ref,
    out_ref,
    gall_ref,
    slot_ref,
    pair_ref,
    slot_row,
    pair_rows,
    index_rows,
    index_ref,
    fields_ref,
    dinter_ref,
    gw_ref,
    contrib,
    total_ref,
    back_ref,
    ids_ref,
    table_ref,
    rows_ref,
    pooled_ref,
    sel_ref,
    sel_t_ref,
    w_ref,
    cot_ref,
    gath,
    part,
    xrecv,
    sa,
    brecv,
    sb,
    crecv,
    gsend,
    grecv,
    bias,
    ag1_s,
    ag1_r,
    ag2_s,
    ag2_r,
    ag3_s,
    ag3_r,
    rs1_s,
    rs1_r,
    rs2_s,
    rs2_r,
    rs3_s,
    rs3_r,
    z_s,
    z_r,
    zb_s,
    zb_r,
    own_sem,
    table_sem,
    a2a_s,
    a2a_r,
    back_s,
    back_r,
    za_s,
    za_r,
):
    nhalf, ny, nx, ncore, per, width = gath.shape
    nrep = gsend.shape[0]
    samples = ny * nx * ncore * per
    hidden = w_ref.shape[1]
    rep, emb = lax.axis_index("rep"), lax.axis_index("emb")
    y, x, c = emb // (nx * ncore), lax.rem(emb // ncore, nx), lax.rem(emb, ncore)

    def at(yy, xx, cc):
        return (rep, (yy * nx + xx) * ncore + cc)

    xs = [lax.rem(x + k, nx) for k in range(nx)]
    ys = [lax.rem(y + k, ny) for k in range(ny)]
    zs = [lax.rem(rep + k, nrep) for k in range(nrep)]
    mate = at(y, x, 1 - c)
    peers = [
        at(ys[dy], xs[dx], lax.rem(c + dc, ncore)) for dy, dx, dc in peer_order(ny, nx, ncore)
    ]
    ndev, ntab, _, embed = rows_ref.shape
    nblocks = fields_ref.shape[0]

    get_ids = pltpu.make_async_copy(ids_hbm, ids_ref, own_sem.at[0])
    get_ids.start()
    small = [
        pltpu.make_async_copy(slot_hbm, slot_ref, own_sem.at[4]),
        pltpu.make_async_copy(pair_hbm, pair_ref, own_sem.at[5]),
        pltpu.make_async_copy(slot_hbm, slot_row.at[0], own_sem.at[6]),
        pltpu.make_async_copy(pair_hbm, pair_rows, own_sem.at[7]),
    ]
    for copy in small:
        copy.start()

    def get_tables(start, size, slot):
        return pltpu.make_async_copy(
            tables_hbm.at[pl.ds(start, size)],
            table_ref.at[slot, pl.ds(0, size)],
            table_sem.at[slot],
        )

    starts = [sum(TABLES[:n]) for n in range(len(TABLES))]
    for n in range(2):
        get_tables(starts[n], TABLES[n], n).start()
    get_w = pltpu.make_async_copy(w_hbm, w_ref, own_sem.at[1])
    get_w.start()
    get_cot = pltpu.make_async_copy(cot_hbm, cot_ref, own_sem.at[2])
    get_cot.start()
    greet(peers)
    greet([(zs[k], emb) for k in range(1, nrep)])
    get_ids.wait()

    def pool_tables(start, size, slot):
        for t in range(size):
            rows = pooled_rows(ids_ref[start + t], len_ref[pl.ds(start + t, 1)], table_ref[slot, t])
            rows_ref[:, start + t] = rows.reshape(ndev, per, embed)

    def send_rows(start, size):
        for _, peer in peers:
            remote(
                rows_ref.at[peer, pl.ds(start, size)],
                pooled_ref.at[pl.ds(emb * ntab + start, size)],
                a2a_s,
                a2a_r,
                (rep, peer),
            ).start()

    for n, size in enumerate(TABLES):
        get_tables(starts[n], size, n % 2).wait()
        pool_tables(starts[n], size, n % 2)
        if n + 2 < len(TABLES):
            get_tables(starts[n + 2], TABLES[n + 2], n % 2).start()
        if n == 0:
            pl.semaphore_wait(pltpu.get_barrier_semaphore(), ndev - 1 + nrep - 1)
        send_rows(starts[n], size)
    own_rows = pltpu.make_async_copy(
        rows_ref.at[emb], pooled_ref.at[pl.ds(emb * ntab, ntab)], own_sem.at[3]
    )
    own_rows.start()
    same = group_masks(per)
    own_cols = own_columns(per)
    sel_ref[...] = select_matrix(per, False)
    sel_t_ref[...] = select_matrix(per, True)
    for copy in small:
        copy.wait()
    order, again, place = scatter_index(pair_rows[...], slot_row[...])
    entries = order.shape[1]
    index_rows[0:1, 0:entries] = order
    index_rows[1:2, 0:entries] = again
    for n, row in enumerate(place):
        index_rows[2:3, n * entries : (n + 1) * entries] = row
    put_index = pltpu.make_async_copy(index_rows, index_ref, own_sem.at[8])
    put_index.start()
    own_rows.wait()
    others = pooled_ref.at[pl.ds(0, (ndev - 1) * ntab)]
    remote(others, others, a2a_s, a2a_r, mate).wait_recv()

    def gather(block, _):
        rows = [
            pooled_ref[slot_ref[block * BLK + i]].astype(jnp.float32) for i in range(BLK)
        ]
        fields_ref[block] = jnp.concatenate(rows, axis=0).astype(jnp.bfloat16)
        return 0

    lax.fori_loop(0, nblocks, gather, 0, unroll=4)

    sent = []

    def send(src, dst, send_sem, recv_sem, device, keep=True):
        copy = remote(src, dst, send_sem, recv_sem, device)
        copy.start()
        if keep:
            sent.append(copy)

    scale = 1.0 / math.sqrt(embed)
    group = GROUP * BLK * BLK
    own = [gath.at[half, y, x, c] for half in range(nhalf)]
    for half in range(nhalf):
        for q in range(width // group):
            first = half * (NPAIR // nhalf) + q * GROUP
            left = jnp.concatenate(
                [fields_ref[pair_ref[0, first + p]] for p in range(GROUP)], axis=0
            )
            right = jnp.concatenate(
                [fields_ref[pair_ref[1, first + p]] for p in range(GROUP)], axis=0
            )
            gram = lax.dot_general(
                left, right, (((1,), (1,)), ((), ())), preferred_element_type=jnp.float32
            )
            gram = jnp.where(same, gram * scale, 0.0).astype(jnp.bfloat16)
            spread = jnp.dot(gram, sel_ref[...], preferred_element_type=jnp.float32)
            kept = jnp.where(own_cols, spread, 0.0).reshape(GROUP * BLK, per, group)
            gath[half, y, x, c, :, q * group : (q + 1) * group] = jnp.sum(kept, axis=0).astype(
                jnp.bfloat16
            )
        for k in range(1, nx):
            near = at(y, xs[k], c) if half == 0 else at(ys[k], x, c)
            far = at(ys[k], x, c) if half == 0 else at(y, xs[k], c)
            send(own[half], own[half], ag1_s.at[half, k], ag1_r.at[half, k], near)
            send(own[half], own[half], ag2_s.at[half, k], ag2_r.at[half, k], far, False)
        send(own[half], own[half], ag3_s.at[half, 0], ag3_r.at[half, 0], mate, False)
    lines = [gath.at[0, y, :, c], gath.at[1, :, x, c]]
    for k in [1, nx - 1] + list(range(2, nx - 1)):
        for half in range(nhalf):
            block = gath.at[0, y, xs[nx - k], c] if half == 0 else gath.at[1, ys[ny - k], x, c]
            remote(block, block, ag1_s.at[half, k], ag1_r.at[half, k], mate).wait_recv()
            for j in range(1, nx):
                far = at(ys[j], x, c) if half == 0 else at(y, xs[j], c)
                send(block, block, ag2_s.at[half, j], ag2_r.at[half, j], far, False)
            send(block, block, ag3_s.at[half, 0], ag3_r.at[half, 0], mate, False)
    for k in [1, nx - 1] + list(range(2, nx - 1)):
        for half in range(nhalf):
            remote(lines[half], lines[half], ag2_s.at[half, k], ag2_r.at[half, k], mate).wait_recv()
            line = gath.at[0, ys[ny - k], :, c] if half == 0 else gath.at[1, :, xs[nx - k], c]
            send(line, line, ag3_s.at[half, k], ag3_r.at[half, k], mate)
    get_w.wait()
    get_cot.wait()
    steps = width // STEP
    pre = jnp.zeros((samples, hidden), jnp.float32)
    for half in range(nhalf):
        for k in range(nx):
            remote(lines[half], lines[half], ag3_s.at[half, k], ag3_r.at[half, k], mate).wait_recv()

        def forward(j, total):
            cols = pl.ds(pl.multiple_of(j * STEP, STEP), STEP)
            rows = pl.ds(pl.multiple_of(half * width + j * STEP, STEP), STEP)
            block = gath[half, :, :, :, :, cols].reshape(samples, STEP)
            return total + jnp.dot(block, w_ref[rows], preferred_element_type=jnp.float32)

        pre = lax.fori_loop(0, steps, forward, pre)
    pre = pre + b_ref[...].astype(jnp.float32)
    sig = jax.nn.sigmoid(pre)
    over_ref[...] = (pre * sig).astype(jnp.bfloat16)
    dpre = (cot_ref[...].astype(jnp.float32) * sig * (1.0 + pre * (1.0 - sig))).astype(jnp.bfloat16)

    for half in range(nhalf):

        def backward(j, _):
            cols = pl.ds(pl.multiple_of(j * STEP, STEP), STEP)
            rows = pl.ds(pl.multiple_of(half * width + j * STEP, STEP), STEP)
            block = lax.dot_general(
                dpre, w_ref[rows], (((1,), (1,)), ((), ())), preferred_element_type=jnp.float32
            )
            block = block.reshape(ny, nx, ncore, per, STEP)
            for core in range(ncore):
                part[half, core, :, :, :, cols] = block[:, :, core].astype(jnp.bfloat16)
            return 0

        lax.fori_loop(0, steps, backward, 0)
        send(part.at[half, 1 - c], xrecv.at[half], rs1_s.at[half], rs1_r.at[half], mate)

    later = [1, nx - 1] + list(range(2, nx - 1)) + [0]
    for half in range(nhalf):
        remote(xrecv.at[half], xrecv.at[half], rs1_s.at[half], rs1_r.at[half], mate).wait_recv()

        def add(j, _):
            sa[half, j] = (
                part[half, c, j].astype(jnp.float32) + xrecv[half, j].astype(jnp.float32)
            ).astype(jnp.bfloat16)
            return 0

        lax.fori_loop(0, ny, add, 0)
        for j in later:
            for k in range(1, nx):
                if half == 0:
                    src, device = sa.at[0, ys[k], xs[j]], at(ys[k], x, c)
                else:
                    src, device = sa.at[1, ys[j], xs[k]], at(y, xs[k], c)
                send(
                    src, brecv.at[half, k - 1, j], rs2_s.at[half, k, j], rs2_r.at[half, k, j], device
                )
    gb = jnp.sum(dpre.astype(jnp.float32), axis=0, keepdims=True)
    bias[rep] = jnp.broadcast_to(gb, bias.shape[1:])
    for k in range(1, nrep):
        send(bias.at[rep], bias.at[rep], zb_s.at[k], zb_r.at[k], (zs[k], emb))
    quarter = gsend.shape[1]
    for half in range(nhalf):

        def weights(j, _):
            cols = pl.ds(pl.multiple_of(j * STEP, STEP), STEP)
            block = gath[half, :, :, :, :, cols].reshape(samples, STEP)
            product = lax.dot_general(
                block, dpre, (((0,), (0,)), ((), ())), preferred_element_type=jnp.float32
            )
            place = half * (width // STEP) + j
            per_quarter = quarter // STEP
            rows = pl.ds(pl.multiple_of(lax.rem(place, per_quarter) * STEP, STEP), STEP)
            gsend[place // per_quarter, rows] = product.astype(jnp.bfloat16)
            return 0

        lax.fori_loop(0, steps, weights, 0)
    for k in range(1, nrep):
        send(gsend.at[zs[k]], grecv.at[k - 1], z_s.at[k], z_r.at[k], (zs[k], emb))

    for j in later:
        for half in range(nhalf):
            place = xs[j] if half == 0 else ys[j]
            mine = sa[0, y, place] if half == 0 else sa[1, place, x]
            total = mine.astype(jnp.float32)
            for k in range(1, nx):
                slot = brecv.at[half, k - 1, j]
                remote(slot, slot, rs2_s.at[half, k, j], rs2_r.at[half, k, j], mate).wait_recv()
                total = total + brecv[half, k - 1, j].astype(jnp.float32)
            sb[half, place] = total.astype(jnp.bfloat16)
            if j:
                device = at(y, xs[j], c) if half == 0 else at(ys[j], x, c)
                send(
                    sb.at[half, place],
                    crecv.at[half, j - 1],
                    rs3_s.at[half, j],
                    rs3_r.at[half, j],
                    device,
                )
    for half in range(nhalf):
        total = sb[half, x if half == 0 else y].astype(jnp.float32)
        for k in range(1, nx):
            slot = crecv.at[half, k - 1]
            remote(slot, slot, rs3_s.at[half, k], rs3_r.at[half, k], mate).wait_recv()
            total = total + crecv[half, k - 1].astype(jnp.float32)
        dinter_ref[:, half * width : (half + 1) * width] = total.astype(jnp.bfloat16)

    put_index.wait()
    for q in range(NPAIR // GROUP):
        left = jnp.concatenate(
            [fields_ref[pair_ref[0, q * GROUP + p]] for p in range(GROUP)], axis=0
        )
        right = jnp.concatenate(
            [fields_ref[pair_ref[1, q * GROUP + p]] for p in range(GROUP)], axis=0
        )
        entry = dinter_ref[:, q * group : (q + 1) * group].astype(jnp.float32)
        spread = jnp.broadcast_to(entry[None], (GROUP * BLK, per, group))
        spread = jnp.where(own_cols, spread.reshape(GROUP * BLK * per, group), 0.0)
        pair = jnp.dot(
            spread.astype(jnp.bfloat16), sel_t_ref[...], preferred_element_type=jnp.float32
        )
        pair = jnp.where(same, pair, 0.0).astype(jnp.bfloat16)
        to_left = jnp.dot(pair, right, preferred_element_type=jnp.float32) * scale
        to_right = (
            lax.dot_general(
                pair, left, (((0,), (0,)), ((), ())), preferred_element_type=jnp.float32
            )
            * scale
        )
        size = (GROUP, BLK * per, embed)
        contrib[q * GROUP : (q + 1) * GROUP] = to_left.reshape(size)
        contrib[NPAIR + q * GROUP : NPAIR + (q + 1) * GROUP] = to_right.reshape(size)

    def run(r, total):
        total = contrib[index_ref[0, r]] + jnp.where(index_ref[1, r] > 0, total, 0.0)
        total_ref[pl.ds(r * BLK, BLK)] = total.reshape(BLK, per, embed)
        return total

    lax.fori_loop(0, 2 * NPAIR, run, jnp.zeros((BLK * per, embed), jnp.float32), unroll=4)

    def fill(device):
        def one(t, _):
            back_ref[device, t] = total_ref[index_ref[2, device * ntab + t]].astype(jnp.bfloat16)
            return 0

        lax.fori_loop(0, ntab, one, 0, unroll=5)

    for _, peer in peers:
        fill(peer)
        remote(back_ref.at[peer], out_ref.at[emb], back_s, back_r, (rep, peer)).start()
    fill(emb)
    own_back = pltpu.make_async_copy(back_ref.at[emb], out_ref.at[emb], own_sem.at[9])
    own_back.start()

    for k in range(1, nrep):
        slot = grecv.at[k - 1]
        remote(slot, slot, z_s.at[k], z_r.at[k], mate).wait_recv()
        remote(bias.at[rep], bias.at[rep], zb_s.at[k], zb_r.at[k], mate).wait_recv()
    total = gsend[rep].astype(jnp.float32)
    for k in range(1, nrep):
        total = total + grecv[k - 1].astype(jnp.float32)
    gw_ref[...] = total.astype(jnp.bfloat16)
    for k in range(1, nrep):
        send(gw_ref, gall_ref.at[rep], za_s.at[k], za_r.at[k], (zs[k], emb))
    own_gw = pltpu.make_async_copy(gw_ref, gall_ref.at[rep], own_sem.at[10])
    own_gw.start()
    gb_ref[...] = jnp.sum(bias[...], axis=0)[:1]

    own_back.wait()
    own_gw.wait()
    for k in range(1, nrep):
        remote(gw_ref, gall_ref.at[0], za_s.at[k], za_r.at[k], mate).wait_recv()
    others = out_ref.at[pl.ds(0, ndev - 1)]
    remote(others, others, back_s, back_r, mate).wait_recv()
    sources = rows_ref.at[pl.ds(0, ndev - 1)]
    remote(sources, sources, a2a_s, a2a_r, mate).wait_send()
    sources = back_ref.at[pl.ds(0, ndev - 1)]
    remote(sources, sources, back_s, back_r, mate).wait_send()
    for half in range(nhalf):
        line = lines[half]
        for k in range(1, nx):
            remote(line, line, ag2_s.at[half, k], ag2_r.at[half, k], mate).wait_send()
        remote(line, line, ag3_s.at[half, 0], ag3_r.at[half, 0], mate).wait_send()
    for copy in sent:
        copy.wait_send()


def train_step(ids, lengths, tables, field_slot, pairs, w, b, cot, grid):
    nrep, ny, nx, ncore = grid
    ndev = ny * nx * ncore
    ntab, bag, samples = ids.shape
    rows, embed = tables.shape[1:]
    per = samples // ndev
    features, hidden = w.shape
    nblocks = ndev * ntab // BLK
    nhalf, width, quarter = 2, features // 2, features // nrep
    half_rows = (nhalf, ny, nx, per, width)
    group = GROUP * BLK * BLK
    dma = pltpu.SemaphoreType.DMA
    bf16 = jnp.bfloat16
    vmem = pl.BlockSpec(memory_space=pltpu.VMEM)
    anywhere = pl.BlockSpec(memory_space=pl.ANY)
    return pl.pallas_call(
        step_kernel,
        in_specs=[anywhere, anywhere, anywhere, vmem, anywhere, anywhere, vmem, anywhere],
        out_specs=[vmem, vmem, anywhere, anywhere],
        out_shape=[
            jax.ShapeDtypeStruct((samples, hidden), bf16),
            jax.ShapeDtypeStruct((1, hidden), jnp.float32),
            jax.ShapeDtypeStruct((ndev, ntab, per, embed), bf16),
            jax.ShapeDtypeStruct((nrep, quarter, hidden), bf16),
        ],
        scratch_shapes=[
            pltpu.SMEM((ndev * ntab,), jnp.int32),
            pltpu.SMEM(pairs.shape, jnp.int32),
            pltpu.VMEM((1, ndev * ntab), jnp.int32),
            pltpu.VMEM(pairs.shape, jnp.int32),
            pltpu.VMEM((8, 1024), jnp.int32),
            pltpu.SMEM((8, 1024), jnp.int32),
            pltpu.VMEM((nblocks, BLK * per, embed), bf16),
            pltpu.VMEM((per, features), bf16),
            pltpu.VMEM((quarter, hidden), bf16),
            pltpu.VMEM((2 * NPAIR, BLK * per, embed), jnp.float32),
            pltpu.VMEM((2 * NPAIR * BLK, per, embed), jnp.float32),
            pltpu.VMEM((ndev, ntab, per, embed), bf16),
            pltpu.VMEM((ntab, bag, samples), jnp.int32),
            pltpu.VMEM((2, max(TABLES), rows, embed), bf16),
            pltpu.VMEM((ndev, ntab, per, embed), bf16),
            pltpu.VMEM((ndev * ntab, per, embed), bf16),
            pltpu.VMEM((group, group), bf16),
            pltpu.VMEM((group, group), bf16),
            pltpu.VMEM((features, hidden), bf16),
            pltpu.VMEM((samples, hidden), bf16),
            pltpu.VMEM((nhalf, ny, nx, ncore, per, width), bf16),
            pltpu.VMEM((nhalf, ncore, ny, nx, per, width), bf16),
            pltpu.VMEM(half_rows, bf16),
            pltpu.VMEM(half_rows, bf16),
            pltpu.VMEM((nhalf, nx - 1, nx, per, width), bf16),
            pltpu.VMEM((nhalf, nx, per, width), bf16),
            pltpu.VMEM((nhalf, nx - 1, per, width), bf16),
            pltpu.VMEM((nrep, quarter, hidden), bf16),
            pltpu.VMEM((nrep - 1, quarter, hidden), bf16),
            pltpu.VMEM((nrep, 8, hidden), jnp.float32),
        ]
        + [dma((nhalf, nx))] * 6
        + [dma((nhalf,))] * 2
        + [dma((nhalf, nx, nx))] * 2
        + [dma((nhalf, nx))] * 2
        + [dma((nrep,))] * 4
        + [dma((11,)), dma((2,)), dma, dma, dma, dma, dma((nrep,)), dma((nrep,))],
        compiler_params=pltpu.CompilerParams(
            vmem_limit_bytes=60 << 20, collective_id=0, has_side_effects=True
        ),
        name="train_step",
    )(
        field_slot,
        pairs,
        ids,
        lengths,
        tables,
        w,
        b.reshape(1, hidden),
        cot,
    )


PARTS = 4


def finish_kernel(
    rows_ref,
    gall_ref,
    over_ref,
    gb_ref,
    pooled_out,
    gw_out,
    over_out,
    gb_out,
    held,
    half,
    full,
    small,
    tiny,
    sems,
):
    nrep, quarter = gall_ref.shape[:2]
    ndev = rows_ref.shape[0]
    size = ndev // PARTS
    first = [pltpu.make_async_copy(gall_ref.at[q], half.at[q], sems.at[0, q]) for q in range(nrep)]
    rows = [
        pltpu.make_async_copy(
            rows_ref.at[pl.ds(g * size, size)], held.at[pl.ds(g * size, size)], sems.at[1, g]
        )
        for g in range(PARTS)
    ]
    extra = [
        pltpu.make_async_copy(over_ref, small, sems.at[4, 0]),
        pltpu.make_async_copy(gb_ref, tiny, sems.at[4, 1]),
    ]
    for copy in [copy for two in zip(rows, first) for copy in two] + extra:
        copy.start()
    out = []
    for g in range(PARTS):
        rows[g].wait()
        for d in range(g * size, (g + 1) * size):
            pltpu.make_async_copy(held.at[d], pooled_out.at[:, d], sems.at[2, 0]).start()
        first[g].wait()
        full[g] = half[g].astype(jnp.float32)
        copy = pltpu.make_async_copy(
            full.at[g], gw_out.at[pl.ds(g * quarter, quarter)], sems.at[3, g]
        )
        copy.start()
        out.append(copy)
    for copy in extra:
        copy.wait()
    last = [
        pltpu.make_async_copy(small, over_out, sems.at[4, 2]),
        pltpu.make_async_copy(tiny, gb_out, sems.at[4, 3]),
    ]
    for copy in last:
        copy.start()
    for copy in last + out:
        copy.wait()
    pltpu.make_async_copy(pooled_out, pooled_out, sems.at[2, 0]).wait()


def finish(rows, gw_all, over, gb):
    ndev, ntab, per, embed = rows.shape
    nrep, quarter, hidden = gw_all.shape
    anywhere = pl.BlockSpec(memory_space=pl.ANY)
    return pl.pallas_call(
        finish_kernel,
        in_specs=[anywhere] * 4,
        out_specs=[anywhere] * 4,
        out_shape=[
            jax.ShapeDtypeStruct((ntab, ndev, per, embed), rows.dtype),
            jax.ShapeDtypeStruct((nrep * quarter, hidden), jnp.float32),
            jax.ShapeDtypeStruct(over.shape, over.dtype),
            jax.ShapeDtypeStruct(gb.shape, gb.dtype),
        ],
        scratch_shapes=[
            pltpu.VMEM(rows.shape, rows.dtype),
            pltpu.VMEM(gw_all.shape, gw_all.dtype),
            pltpu.VMEM(gw_all.shape, jnp.float32),
            pltpu.VMEM(over.shape, over.dtype),
            pltpu.VMEM(gb.shape, gb.dtype),
            pltpu.SemaphoreType.DMA((5, nrep)),
        ],
        compiler_params=pltpu.CompilerParams(vmem_limit_bytes=60 << 20),
        name="finish",
    )(rows, gw_all, over, gb)


def on_device(tables, bag_ids, bag_lengths, field_slot, pair_blocks, w_over, b_over, cotangent):
    grid = (lax.axis_size("rep"), 4, 4, 2)
    ids, pairs = jnp.swapaxes(bag_ids, 1, 2), pair_blocks.T
    over, gb, rows, gw_all = train_step(
        ids, bag_lengths, tables, field_slot, pairs, w_over, b_over, cotangent, grid
    )
    pooled_grad, grad_w, over_out, grad_b = finish(rows, gw_all, over, gb)
    return (
        over_out,
        grad_w,
        grad_b.reshape(b_over.shape),
        pooled_grad.reshape(tables.shape[0], bag_ids.shape[1], tables.shape[2]),
    )


def solution(mesh):
    in_specs = (
        P("emb", None, None),
        P("emb", "rep", None),
        P("emb", "rep"),
        P(),
        P(),
        P(None, "emb"),
        P("emb"),
        P("rep", "emb"),
    )
    out_specs = (P("rep", "emb"), P(None, "emb"), P("emb"), P("emb", "rep", None))
    return jax.shard_map(
        on_device, mesh=mesh, in_specs=in_specs, out_specs=out_specs, check_vma=False
    )
```

```python
import functools
import math

import jax
import jax.numpy as jnp
from jax import lax
from jax.experimental import pallas as pl
from jax.experimental.pallas import tpu as pltpu
from jax.sharding import PartitionSpec as P

BLK = 8
NPAIR = 64
GROUP = 4
WORDS = 128
BITS = 4
NIBBLES = 0x0F0F0F0F


MESH = pl.DeviceIdType.MESH
TABLES = (6, 8, 7, 4)


def remote(src, dst, send_sem, recv_sem, device):
    return pltpu.make_async_remote_copy(
        src_ref=src,
        dst_ref=dst,
        send_sem=send_sem,
        recv_sem=recv_sem,
        device_id=device,
        device_id_type=MESH,
    )


def greet(devices):
    barrier = pltpu.get_barrier_semaphore()
    for device in devices:
        pl.semaphore_signal(barrier, inc=1, device_id=device, device_id_type=MESH)


def peer_order(ny, nx, ncore):
    left = [
        (dy, dx, dc)
        for dy in range(ny)
        for dx in range(nx)
        for dc in range(ncore)
        if (dy, dx, dc) != (0, 0, 0)
    ]

    def links(offset):
        used = []
        for axis, (step, size) in enumerate(((offset[0], ny), (offset[1], nx))):
            if 0 < step <= size // 2:
                used.append(2 * axis)
            if step >= size - size // 2 and step > 0:
                used.append(2 * axis + 1)
        return used

    order, load = [], [0] * 4

    def cost(offset):
        after = list(load)
        for link in links(offset):
            after[link] += 1
        return max(after) - min(after)

    while left:
        best = min(left, key=cost)
        left.remove(best)
        order.append(best)
        for link in links(best):
            load[link] += 1
    return order


def pooled_rows(ids, lengths, table):
    bag, samples = ids.shape
    used = lax.broadcasted_iota(jnp.int32, (bag, samples), 0) < lengths
    word = ids & (WORDS - 1)
    value = jnp.where(used, jnp.left_shift(1, (ids // WORDS) * BITS), 0)
    lows, highs = [], []
    for half in range(samples // 128):
        lanes = slice(half * 128, half * 128 + 128)
        row = lax.broadcasted_iota(jnp.int32, (WORDS, 128), 0)
        low, high = None, None
        for first in range(0, bag, 8):
            total = None
            for k in range(first, first + 8):
                hit = jnp.where(row == word[k : k + 1, lanes], value[k : k + 1, lanes], 0)
                total = hit if total is None else total + hit
            even, odd = total & NIBBLES, (total >> BITS) & NIBBLES
            low = even if low is None else low + even
            high = odd if high is None else high + odd
        lows.append(low)
        highs.append(high)
    bytes_of = [jnp.concatenate(lows, axis=1), jnp.concatenate(highs, axis=1)]
    chunks = []
    for part in range(table.shape[0] // WORDS):
        chunk = (bytes_of[part % 2] >> (8 * (part // 2))) & 31
        chunks.append(chunk.astype(jnp.float32).astype(jnp.bfloat16))
    pooled = lax.dot_general(
        table,
        jnp.concatenate(chunks, axis=0),
        (((0,), (0,)), ((), ())),
        preferred_element_type=jnp.float32,
    )
    return pooled.T.astype(jnp.bfloat16)


def group_masks(samples):
    n = GROUP * BLK * samples
    r = lax.broadcasted_iota(jnp.int32, (n, n), 0)
    c = lax.broadcasted_iota(jnp.int32, (n, n), 1)
    per = BLK * samples
    same = (r // per == c // per) & (r % samples == c % samples)
    return same


def select_matrix(samples, transposed):
    rows, cols = GROUP * BLK * samples, GROUP * BLK * BLK
    shape = (cols, rows) if transposed else (rows, cols)
    r = lax.broadcasted_iota(jnp.int32, shape, 1 if transposed else 0)
    c = lax.broadcasted_iota(jnp.int32, shape, 0 if transposed else 1)
    hit = (r // (BLK * samples) == c // (BLK * BLK)) & ((r // samples) % BLK == c % BLK)
    return jnp.where(hit, 1.0, 0.0).astype(jnp.bfloat16)


def own_columns(samples):
    rows, cols = GROUP * BLK * samples, GROUP * BLK * BLK
    r = lax.broadcasted_iota(jnp.int32, (rows, cols), 0)
    c = lax.broadcasted_iota(jnp.int32, (rows, cols), 1)
    return r // samples == c // BLK


STEP = 512


def scatter_index(pair_rows, slots):
    entries, nfields = 2 * pair_rows.shape[1], slots.shape[1]
    block = jnp.concatenate([pair_rows[0:1], pair_rows[1:2]], axis=1)
    square = (entries, entries)
    down = lax.broadcasted_iota(jnp.int32, square, 0)
    across = lax.broadcasted_iota(jnp.int32, square, 1)
    of_col = jnp.broadcast_to(block, square)
    of_row = of_col.T
    earlier = (of_row == of_col) & (down < across)
    rank = jnp.sum(jnp.where((of_row < of_col) | earlier, 1, 0), axis=0, keepdims=True)
    repeat = jnp.sum(jnp.where(earlier, 1, 0), axis=0, keepdims=True)
    hit = jnp.broadcast_to(rank, square).T == across
    order = jnp.sum(jnp.where(hit, down, 0), axis=0, keepdims=True)
    again = jnp.sum(jnp.where(hit, jnp.broadcast_to(repeat, square).T, 0), axis=0, keepdims=True)

    wide = (entries, nfields)
    own_block = lax.broadcasted_iota(jnp.int32, wide, 1) // BLK
    upto = jnp.where(of_row[:, :1] <= own_block, 1, 0)
    last = jnp.sum(upto, axis=0, keepdims=True) - 1
    piece = last * BLK + lax.broadcasted_iota(jnp.int32, (1, nfields), 1) % BLK
    places = []
    for start in range(0, nfields, entries):
        slot = lax.broadcasted_iota(jnp.int32, wide, 0) + start
        found = jnp.sum(jnp.where(slot == slots, piece, 0), axis=1, keepdims=True)
        row = jnp.broadcast_to(found, square).T
        places.append(jnp.clip(row[0:1], 0, entries * BLK - 1))
    return jnp.clip(order, 0, entries - 1), again, places


def step_kernel(
    slot_hbm,
    pair_hbm,
    ids_hbm,
    len_ref,
    tables_hbm,
    w_hbm,
    b_ref,
    cot_hbm,
    over_ref,
    gb_ref,
    out_ref,
    gall_ref,
    slot_ref,
    pair_ref,
    slot_row,
    pair_rows,
    index_rows,
    index_ref,
    fields_ref,
    dinter_ref,
    gw_ref,
    contrib,
    total_ref,
    back_ref,
    ids_ref,
    table_ref,
    rows_ref,
    pooled_ref,
    sel_ref,
    sel_t_ref,
    w_ref,
    cot_ref,
    gath,
    part,
    xrecv,
    sa,
    brecv,
    sb,
    crecv,
    gsend,
    grecv,
    bias,
    ag1_s,
    ag1_r,
    ag2_s,
    ag2_r,
    ag3_s,
    ag3_r,
    rs1_s,
    rs1_r,
    rs2_s,
    rs2_r,
    rs3_s,
    rs3_r,
    z_s,
    z_r,
    zb_s,
    zb_r,
    own_sem,
    table_sem,
    a2a_s,
    a2a_r,
    back_s,
    back_r,
    za_s,
    za_r,
):
    nhalf, ny, nx, ncore, per, width = gath.shape
    nrep = gsend.shape[0]
    samples = ny * nx * ncore * per
    hidden = w_ref.shape[1]
    rep, emb = lax.axis_index("rep"), lax.axis_index("emb")
    y, x, c = emb // (nx * ncore), lax.rem(emb // ncore, nx), lax.rem(emb, ncore)

    def at(yy, xx, cc):
        return (rep, (yy * nx + xx) * ncore + cc)

    xs = [lax.rem(x + k, nx) for k in range(nx)]
    ys = [lax.rem(y + k, ny) for k in range(ny)]
    zs = [lax.rem(rep + k, nrep) for k in range(nrep)]
    mate = at(y, x, 1 - c)
    peers = [
        at(ys[dy], xs[dx], lax.rem(c + dc, ncore)) for dy, dx, dc in peer_order(ny, nx, ncore)
    ]
    ndev, ntab, _, embed = rows_ref.shape
    nblocks = fields_ref.shape[0]

    get_ids = pltpu.make_async_copy(ids_hbm, ids_ref, own_sem.at[0])
    get_ids.start()
    small = [
        pltpu.make_async_copy(slot_hbm, slot_ref, own_sem.at[4]),
        pltpu.make_async_copy(pair_hbm, pair_ref, own_sem.at[5]),
        pltpu.make_async_copy(slot_hbm, slot_row.at[0], own_sem.at[6]),
        pltpu.make_async_copy(pair_hbm, pair_rows, own_sem.at[7]),
    ]
    for copy in small:
        copy.start()

    def get_tables(start, size, slot):
        return pltpu.make_async_copy(
            tables_hbm.at[pl.ds(start, size)],
            table_ref.at[slot, pl.ds(0, size)],
            table_sem.at[slot],
        )

    starts = [sum(TABLES[:n]) for n in range(len(TABLES))]
    for n in range(2):
        get_tables(starts[n], TABLES[n], n).start()
    get_w = pltpu.make_async_copy(w_hbm, w_ref, own_sem.at[1])
    get_w.start()
    get_cot = pltpu.make_async_copy(cot_hbm, cot_ref, own_sem.at[2])
    get_cot.start()
    greet(peers)
    greet([(zs[k], emb) for k in range(1, nrep)])
    get_ids.wait()

    def pool_tables(start, size, slot):
        for t in range(size):
            rows = pooled_rows(ids_ref[start + t], len_ref[pl.ds(start + t, 1)], table_ref[slot, t])
            rows_ref[:, start + t] = rows.reshape(ndev, per, embed)

    def send_rows(start, size):
        for _, peer in peers:
            remote(
                rows_ref.at[peer, pl.ds(start, size)],
                pooled_ref.at[pl.ds(emb * ntab + start, size)],
                a2a_s,
                a2a_r,
                (rep, peer),
            ).start()

    for n, size in enumerate(TABLES):
        get_tables(starts[n], size, n % 2).wait()
        pool_tables(starts[n], size, n % 2)
        if n + 2 < len(TABLES):
            get_tables(starts[n + 2], TABLES[n + 2], n % 2).start()
        if n == 0:
            pl.semaphore_wait(pltpu.get_barrier_semaphore(), ndev - 1 + nrep - 1)
        send_rows(starts[n], size)
    own_rows = pltpu.make_async_copy(
        rows_ref.at[emb], pooled_ref.at[pl.ds(emb * ntab, ntab)], own_sem.at[3]
    )
    own_rows.start()
    same = group_masks(per)
    own_cols = own_columns(per)
    sel_ref[...] = select_matrix(per, False)
    sel_t_ref[...] = select_matrix(per, True)
    for copy in small:
        copy.wait()
    order, again, place = scatter_index(pair_rows[...], slot_row[...])
    entries = order.shape[1]
    index_rows[0:1, 0:entries] = order
    index_rows[1:2, 0:entries] = again
    for n, row in enumerate(place):
        index_rows[2:3, n * entries : (n + 1) * entries] = row
    put_index = pltpu.make_async_copy(index_rows, index_ref, own_sem.at[8])
    put_index.start()
    own_rows.wait()
    others = pooled_ref.at[pl.ds(0, (ndev - 1) * ntab)]
    remote(others, others, a2a_s, a2a_r, mate).wait_recv()

    def gather(block, _):
        rows = [
            pooled_ref[slot_ref[block * BLK + i]].astype(jnp.float32) for i in range(BLK)
        ]
        fields_ref[block] = jnp.concatenate(rows, axis=0).astype(jnp.bfloat16)
        return 0

    lax.fori_loop(0, nblocks, gather, 0, unroll=4)

    sent = []

    def send(src, dst, send_sem, recv_sem, device, keep=True):
        copy = remote(src, dst, send_sem, recv_sem, device)
        copy.start()
        if keep:
            sent.append(copy)

    scale = 1.0 / math.sqrt(embed)
    group = GROUP * BLK * BLK
    own = [gath.at[half, y, x, c] for half in range(nhalf)]
    for half in range(nhalf):
        for q in range(width // group):
            first = half * (NPAIR // nhalf) + q * GROUP
            left = jnp.concatenate(
                [fields_ref[pair_ref[0, first + p]] for p in range(GROUP)], axis=0
            )
            right = jnp.concatenate(
                [fields_ref[pair_ref[1, first + p]] for p in range(GROUP)], axis=0
            )
            gram = lax.dot_general(
                left, right, (((1,), (1,)), ((), ())), preferred_element_type=jnp.float32
            )
            gram = jnp.where(same, gram * scale, 0.0).astype(jnp.bfloat16)
            spread = jnp.dot(gram, sel_ref[...], preferred_element_type=jnp.float32)
            kept = jnp.where(own_cols, spread, 0.0).reshape(GROUP * BLK, per, group)
            gath[half, y, x, c, :, q * group : (q + 1) * group] = jnp.sum(kept, axis=0).astype(
                jnp.bfloat16
            )
        for k in range(1, nx):
            near = at(y, xs[k], c) if half == 0 else at(ys[k], x, c)
            far = at(ys[k], x, c) if half == 0 else at(y, xs[k], c)
            send(own[half], own[half], ag1_s.at[half, k], ag1_r.at[half, k], near)
            send(own[half], own[half], ag2_s.at[half, k], ag2_r.at[half, k], far, False)
        send(own[half], own[half], ag3_s.at[half, 0], ag3_r.at[half, 0], mate, False)
    lines = [gath.at[0, y, :, c], gath.at[1, :, x, c]]
    for k in [1, nx - 1] + list(range(2, nx - 1)):
        for half in range(nhalf):
            block = gath.at[0, y, xs[nx - k], c] if half == 0 else gath.at[1, ys[ny - k], x, c]
            remote(block, block, ag1_s.at[half, k], ag1_r.at[half, k], mate).wait_recv()
            for j in range(1, nx):
                far = at(ys[j], x, c) if half == 0 else at(y, xs[j], c)
                send(block, block, ag2_s.at[half, j], ag2_r.at[half, j], far, False)
            send(block, block, ag3_s.at[half, 0], ag3_r.at[half, 0], mate, False)
    for k in [1, nx - 1] + list(range(2, nx - 1)):
        for half in range(nhalf):
            remote(lines[half], lines[half], ag2_s.at[half, k], ag2_r.at[half, k], mate).wait_recv()
            line = gath.at[0, ys[ny - k], :, c] if half == 0 else gath.at[1, :, xs[nx - k], c]
            send(line, line, ag3_s.at[half, k], ag3_r.at[half, k], mate)
    get_w.wait()
    get_cot.wait()
    steps = width // STEP
    pre = jnp.zeros((samples, hidden), jnp.float32)
    for half in range(nhalf):
        for k in range(nx):
            remote(lines[half], lines[half], ag3_s.at[half, k], ag3_r.at[half, k], mate).wait_recv()

        def forward(j, total):
            cols = pl.ds(pl.multiple_of(j * STEP, STEP), STEP)
            rows = pl.ds(pl.multiple_of(half * width + j * STEP, STEP), STEP)
            block = gath[half, :, :, :, :, cols].reshape(samples, STEP)
            return total + jnp.dot(block, w_ref[rows], preferred_element_type=jnp.float32)

        pre = lax.fori_loop(0, steps, forward, pre)
    pre = pre + b_ref[...].astype(jnp.float32)
    sig = jax.nn.sigmoid(pre)
    over_ref[...] = (pre * sig).astype(jnp.bfloat16)
    dpre = (cot_ref[...].astype(jnp.float32) * sig * (1.0 + pre * (1.0 - sig))).astype(jnp.bfloat16)

    for half in range(nhalf):

        def backward(j, _):
            cols = pl.ds(pl.multiple_of(j * STEP, STEP), STEP)
            rows = pl.ds(pl.multiple_of(half * width + j * STEP, STEP), STEP)
            block = lax.dot_general(
                dpre, w_ref[rows], (((1,), (1,)), ((), ())), preferred_element_type=jnp.float32
            )
            block = block.reshape(ny, nx, ncore, per, STEP)
            for core in range(ncore):
                part[half, core, :, :, :, cols] = block[:, :, core].astype(jnp.bfloat16)
            return 0

        lax.fori_loop(0, steps, backward, 0)
        send(part.at[half, 1 - c], xrecv.at[half], rs1_s.at[half], rs1_r.at[half], mate)

    later = [1, nx - 1] + list(range(2, nx - 1)) + [0]
    for half in range(nhalf):
        remote(xrecv.at[half], xrecv.at[half], rs1_s.at[half], rs1_r.at[half], mate).wait_recv()

        def add(j, _):
            sa[half, j] = (
                part[half, c, j].astype(jnp.float32) + xrecv[half, j].astype(jnp.float32)
            ).astype(jnp.bfloat16)
            return 0

        lax.fori_loop(0, ny, add, 0)
        for j in later:
            for k in range(1, nx):
                if half == 0:
                    src, device = sa.at[0, ys[k], xs[j]], at(ys[k], x, c)
                else:
                    src, device = sa.at[1, ys[j], xs[k]], at(y, xs[k], c)
                send(
                    src, brecv.at[half, k - 1, j], rs2_s.at[half, k, j], rs2_r.at[half, k, j], device
                )
    gb = jnp.sum(dpre.astype(jnp.float32), axis=0, keepdims=True)
    bias[rep] = jnp.broadcast_to(gb, bias.shape[1:])
    for k in range(1, nrep):
        send(bias.at[rep], bias.at[rep], zb_s.at[k], zb_r.at[k], (zs[k], emb))
    quarter = gsend.shape[1]
    for half in range(nhalf):

        def weights(j, _):
            cols = pl.ds(pl.multiple_of(j * STEP, STEP), STEP)
            block = gath[half, :, :, :, :, cols].reshape(samples, STEP)
            product = lax.dot_general(
                block, dpre, (((0,), (0,)), ((), ())), preferred_element_type=jnp.float32
            )
            place = half * (width // STEP) + j
            per_quarter = quarter // STEP
            rows = pl.ds(pl.multiple_of(lax.rem(place, per_quarter) * STEP, STEP), STEP)
            gsend[place // per_quarter, rows] = product.astype(jnp.bfloat16)
            return 0

        lax.fori_loop(0, steps, weights, 0)
    for k in range(1, nrep):
        send(gsend.at[zs[k]], grecv.at[k - 1], z_s.at[k], z_r.at[k], (zs[k], emb))

    for j in later:
        for half in range(nhalf):
            place = xs[j] if half == 0 else ys[j]
            mine = sa[0, y, place] if half == 0 else sa[1, place, x]
            total = mine.astype(jnp.float32)
            for k in range(1, nx):
                slot = brecv.at[half, k - 1, j]
                remote(slot, slot, rs2_s.at[half, k, j], rs2_r.at[half, k, j], mate).wait_recv()
                total = total + brecv[half, k - 1, j].astype(jnp.float32)
            sb[half, place] = total.astype(jnp.bfloat16)
            if j:
                device = at(y, xs[j], c) if half == 0 else at(ys[j], x, c)
                send(
                    sb.at[half, place],
                    crecv.at[half, j - 1],
                    rs3_s.at[half, j],
                    rs3_r.at[half, j],
                    device,
                )
    for half in range(nhalf):
        total = sb[half, x if half == 0 else y].astype(jnp.float32)
        for k in range(1, nx):
            slot = crecv.at[half, k - 1]
            remote(slot, slot, rs3_s.at[half, k], rs3_r.at[half, k], mate).wait_recv()
            total = total + crecv[half, k - 1].astype(jnp.float32)
        dinter_ref[:, half * width : (half + 1) * width] = total.astype(jnp.bfloat16)

    put_index.wait()
    for q in range(NPAIR // GROUP):
        left = jnp.concatenate(
            [fields_ref[pair_ref[0, q * GROUP + p]] for p in range(GROUP)], axis=0
        )
        right = jnp.concatenate(
            [fields_ref[pair_ref[1, q * GROUP + p]] for p in range(GROUP)], axis=0
        )
        entry = dinter_ref[:, q * group : (q + 1) * group].astype(jnp.float32)
        spread = jnp.broadcast_to(entry[None], (GROUP * BLK, per, group))
        spread = jnp.where(own_cols, spread.reshape(GROUP * BLK * per, group), 0.0)
        pair = jnp.dot(
            spread.astype(jnp.bfloat16), sel_t_ref[...], preferred_element_type=jnp.float32
        )
        pair = jnp.where(same, pair, 0.0).astype(jnp.bfloat16)
        to_left = jnp.dot(pair, right, preferred_element_type=jnp.float32) * scale
        to_right = (
            lax.dot_general(
                pair, left, (((0,), (0,)), ((), ())), preferred_element_type=jnp.float32
            )
            * scale
        )
        size = (GROUP, BLK * per, embed)
        contrib[q * GROUP : (q + 1) * GROUP] = to_left.reshape(size)
        contrib[NPAIR + q * GROUP : NPAIR + (q + 1) * GROUP] = to_right.reshape(size)

    def run(r, total):
        total = contrib[index_ref[0, r]] + jnp.where(index_ref[1, r] > 0, total, 0.0)
        total_ref[pl.ds(r * BLK, BLK)] = total.reshape(BLK, per, embed)
        return total

    lax.fori_loop(0, 2 * NPAIR, run, jnp.zeros((BLK * per, embed), jnp.float32), unroll=4)

    def fill(device):
        def one(t, _):
            back_ref[device, t] = total_ref[index_ref[2, device * ntab + t]].astype(jnp.bfloat16)
            return 0

        lax.fori_loop(0, ntab, one, 0, unroll=5)

    def gather_weights():
        for k in range(1, nrep):
            slot = grecv.at[k - 1]
            remote(slot, slot, z_s.at[k], z_r.at[k], mate).wait_recv()
            remote(bias.at[rep], bias.at[rep], zb_s.at[k], zb_r.at[k], mate).wait_recv()
        total = gsend[rep].astype(jnp.float32)
        for k in range(1, nrep):
            total = total + grecv[k - 1].astype(jnp.float32)
        gw_ref[...] = total.astype(jnp.bfloat16)
        for k in range(1, nrep):
            send(gw_ref, gall_ref.at[rep], za_s.at[k], za_r.at[k], (zs[k], emb))
        own_gw = pltpu.make_async_copy(gw_ref, gall_ref.at[rep], own_sem.at[10])
        own_gw.start()
        return own_gw

    for n, (_, peer) in enumerate(peers):
        if n == 8:
            own_gw = gather_weights()
        fill(peer)
        remote(back_ref.at[peer], out_ref.at[emb], back_s, back_r, (rep, peer)).start()
    fill(emb)
    own_back = pltpu.make_async_copy(back_ref.at[emb], out_ref.at[emb], own_sem.at[9])
    own_back.start()

    gb_ref[...] = jnp.sum(bias[...], axis=0)[:1]

    own_back.wait()
    own_gw.wait()
    for k in range(1, nrep):
        remote(gw_ref, gall_ref.at[0], za_s.at[k], za_r.at[k], mate).wait_recv()
    others = out_ref.at[pl.ds(0, ndev - 1)]
    remote(others, others, back_s, back_r, mate).wait_recv()
    sources = rows_ref.at[pl.ds(0, ndev - 1)]
    remote(sources, sources, a2a_s, a2a_r, mate).wait_send()
    sources = back_ref.at[pl.ds(0, ndev - 1)]
    remote(sources, sources, back_s, back_r, mate).wait_send()
    for half in range(nhalf):
        line = lines[half]
        for k in range(1, nx):
            remote(line, line, ag2_s.at[half, k], ag2_r.at[half, k], mate).wait_send()
        remote(line, line, ag3_s.at[half, 0], ag3_r.at[half, 0], mate).wait_send()
    for copy in sent:
        copy.wait_send()


def train_step(ids, lengths, tables, field_slot, pairs, w, b, cot, grid):
    nrep, ny, nx, ncore = grid
    ndev = ny * nx * ncore
    ntab, bag, samples = ids.shape
    rows, embed = tables.shape[1:]
    per = samples // ndev
    features, hidden = w.shape
    nblocks = ndev * ntab // BLK
    nhalf, width, quarter = 2, features // 2, features // nrep
    half_rows = (nhalf, ny, nx, per, width)
    group = GROUP * BLK * BLK
    dma = pltpu.SemaphoreType.DMA
    bf16 = jnp.bfloat16
    vmem = pl.BlockSpec(memory_space=pltpu.VMEM)
    anywhere = pl.BlockSpec(memory_space=pl.ANY)
    return pl.pallas_call(
        step_kernel,
        in_specs=[anywhere, anywhere, anywhere, vmem, anywhere, anywhere, vmem, anywhere],
        out_specs=[vmem, vmem, anywhere, anywhere],
        out_shape=[
            jax.ShapeDtypeStruct((samples, hidden), bf16),
            jax.ShapeDtypeStruct((1, hidden), jnp.float32),
            jax.ShapeDtypeStruct((ndev, ntab, per, embed), bf16),
            jax.ShapeDtypeStruct((nrep, quarter, hidden), bf16),
        ],
        scratch_shapes=[
            pltpu.SMEM((ndev * ntab,), jnp.int32),
            pltpu.SMEM(pairs.shape, jnp.int32),
            pltpu.VMEM((1, ndev * ntab), jnp.int32),
            pltpu.VMEM(pairs.shape, jnp.int32),
            pltpu.VMEM((8, 1024), jnp.int32),
            pltpu.SMEM((8, 1024), jnp.int32),
            pltpu.VMEM((nblocks, BLK * per, embed), bf16),
            pltpu.VMEM((per, features), bf16),
            pltpu.VMEM((quarter, hidden), bf16),
            pltpu.VMEM((2 * NPAIR, BLK * per, embed), jnp.float32),
            pltpu.VMEM((2 * NPAIR * BLK, per, embed), jnp.float32),
            pltpu.VMEM((ndev, ntab, per, embed), bf16),
            pltpu.VMEM((ntab, bag, samples), jnp.int32),
            pltpu.VMEM((2, max(TABLES), rows, embed), bf16),
            pltpu.VMEM((ndev, ntab, per, embed), bf16),
            pltpu.VMEM((ndev * ntab, per, embed), bf16),
            pltpu.VMEM((group, group), bf16),
            pltpu.VMEM((group, group), bf16),
            pltpu.VMEM((features, hidden), bf16),
            pltpu.VMEM((samples, hidden), bf16),
            pltpu.VMEM((nhalf, ny, nx, ncore, per, width), bf16),
            pltpu.VMEM((nhalf, ncore, ny, nx, per, width), bf16),
            pltpu.VMEM(half_rows, bf16),
            pltpu.VMEM(half_rows, bf16),
            pltpu.VMEM((nhalf, nx - 1, nx, per, width), bf16),
            pltpu.VMEM((nhalf, nx, per, width), bf16),
            pltpu.VMEM((nhalf, nx - 1, per, width), bf16),
            pltpu.VMEM((nrep, quarter, hidden), bf16),
            pltpu.VMEM((nrep - 1, quarter, hidden), bf16),
            pltpu.VMEM((nrep, 8, hidden), jnp.float32),
        ]
        + [dma((nhalf, nx))] * 6
        + [dma((nhalf,))] * 2
        + [dma((nhalf, nx, nx))] * 2
        + [dma((nhalf, nx))] * 2
        + [dma((nrep,))] * 4
        + [dma((11,)), dma((2,)), dma, dma, dma, dma, dma((nrep,)), dma((nrep,))],
        compiler_params=pltpu.CompilerParams(
            vmem_limit_bytes=60 << 20, collective_id=0, has_side_effects=True
        ),
        name="train_step",
    )(
        field_slot,
        pairs,
        ids,
        lengths,
        tables,
        w,
        b.reshape(1, hidden),
        cot,
    )


PARTS = 4


def finish_kernel(
    rows_ref,
    gall_ref,
    over_ref,
    gb_ref,
    pooled_out,
    gw_out,
    over_out,
    gb_out,
    held,
    half,
    full,
    small,
    tiny,
    sems,
):
    nrep, quarter = gall_ref.shape[:2]
    ndev = rows_ref.shape[0]
    size = ndev // PARTS
    first = [pltpu.make_async_copy(gall_ref.at[q], half.at[q], sems.at[0, q]) for q in range(nrep)]
    rows = [
        pltpu.make_async_copy(
            rows_ref.at[pl.ds(g * size, size)], held.at[pl.ds(g * size, size)], sems.at[1, g]
        )
        for g in range(PARTS)
    ]
    extra = [
        pltpu.make_async_copy(over_ref, small, sems.at[4, 0]),
        pltpu.make_async_copy(gb_ref, tiny, sems.at[4, 1]),
    ]
    for copy in [copy for two in zip(rows, first) for copy in two] + extra:
        copy.start()
    out = []
    for g in range(PARTS):
        rows[g].wait()
        for d in range(g * size, (g + 1) * size):
            pltpu.make_async_copy(held.at[d], pooled_out.at[:, d], sems.at[2, 0]).start()
        first[g].wait()
        full[g] = half[g].astype(jnp.float32)
        copy = pltpu.make_async_copy(
            full.at[g], gw_out.at[pl.ds(g * quarter, quarter)], sems.at[3, g]
        )
        copy.start()
        out.append(copy)
    for copy in extra:
        copy.wait()
    last = [
        pltpu.make_async_copy(small, over_out, sems.at[4, 2]),
        pltpu.make_async_copy(tiny, gb_out, sems.at[4, 3]),
    ]
    for copy in last:
        copy.start()
    for copy in last + out:
        copy.wait()
    pltpu.make_async_copy(pooled_out, pooled_out, sems.at[2, 0]).wait()


def finish(rows, gw_all, over, gb):
    ndev, ntab, per, embed = rows.shape
    nrep, quarter, hidden = gw_all.shape
    anywhere = pl.BlockSpec(memory_space=pl.ANY)
    return pl.pallas_call(
        finish_kernel,
        in_specs=[anywhere] * 4,
        out_specs=[anywhere] * 4,
        out_shape=[
            jax.ShapeDtypeStruct((ntab, ndev, per, embed), rows.dtype),
            jax.ShapeDtypeStruct((nrep * quarter, hidden), jnp.float32),
            jax.ShapeDtypeStruct(over.shape, over.dtype),
            jax.ShapeDtypeStruct(gb.shape, gb.dtype),
        ],
        scratch_shapes=[
            pltpu.VMEM(rows.shape, rows.dtype),
            pltpu.VMEM(gw_all.shape, gw_all.dtype),
            pltpu.VMEM(gw_all.shape, jnp.float32),
            pltpu.VMEM(over.shape, over.dtype),
            pltpu.VMEM(gb.shape, gb.dtype),
            pltpu.SemaphoreType.DMA((5, nrep)),
        ],
        compiler_params=pltpu.CompilerParams(vmem_limit_bytes=60 << 20),
        name="finish",
    )(rows, gw_all, over, gb)


def on_device(tables, bag_ids, bag_lengths, field_slot, pair_blocks, w_over, b_over, cotangent):
    grid = (lax.axis_size("rep"), 4, 4, 2)
    ids, pairs = jnp.swapaxes(bag_ids, 1, 2), pair_blocks.T
    over, gb, rows, gw_all = train_step(
        ids, bag_lengths, tables, field_slot, pairs, w_over, b_over, cotangent, grid
    )
    pooled_grad, grad_w, over_out, grad_b = finish(rows, gw_all, over, gb)
    return (
        over_out,
        grad_w,
        grad_b.reshape(b_over.shape),
        pooled_grad.reshape(tables.shape[0], bag_ids.shape[1], tables.shape[2]),
    )


def solution(mesh):
    in_specs = (
        P("emb", None, None),
        P("emb", "rep", None),
        P("emb", "rep"),
        P(),
        P(),
        P(None, "emb"),
        P("emb"),
        P("rep", "emb"),
    )
    out_specs = (P("rep", "emb"), P(None, "emb"), P("emb"), P("emb", "rep", None))
    return jax.shard_map(
        on_device, mesh=mesh, in_specs=in_specs, out_specs=out_specs, check_vma=False
    )
```
